32 devices in a mesh: section: 1, expert: 32 (over z, y, x, core).
Axes of the slice: x: 2, y: 2, z: 4, core: 2. Of those that a mesh axis runs over, the one named last changes fastest.
Arguments:
- forward_input: bfloat16 [1, 3072, 1024], P('section', 'expert'), may hold values from -6 to 6
- forward_routes: int32 [1, 3072, 6], P('section', 'expert'), may hold values from 0 to 15, all different within a row; in each aligned block of 96 rows (0 to 95, 96 to 191, ..., all dimensions but the last counted through in order) at most 42 rows name the same one
- forward_gates: float32 [1, 3072, 6], P('section', 'expert'), may hold values from 0.05 to 0.6
- backward_input: bfloat16 [1, 1536, 1024], P('section', 'expert'), may hold values from -6 to 6
- backward_routes: int32 [1, 1536, 6], P('section', 'expert'), may hold values from 0 to 15, all different within a row; in each aligned block of 48 rows (0 to 47, 48 to 95, ..., all dimensions but the last counted through in order) at most 20 rows name the same one
- backward_gates: float32 [1, 1536, 6], P('section', 'expert'), may hold values from 0.05 to 0.6
- output_grad: bfloat16 [1, 1536, 1024], P('section', 'expert'), may hold values from -6 to 6
- weight_in: bfloat16 [1, 32, 1024, 1024], P('section', 'expert'), may hold values from -0.1875 to 0.1875
- weight_down: bfloat16 [1, 32, 512, 1024], P('section', 'expert'), may hold values from -0.1875 to 0.1875
Outputs:
- forward_sent: bfloat16 [1, 3072, 1024], P('section', 'expert')
- backward_sent: bfloat16 [1, 1536, 1024], P('section', 'expert')
The draws below stay inside these ranges and needn't reach their ends.
Inputs may be any that keep to these rules, and one draw needn't show every extreme that they name: `forward_routes`: each row names 6 different experts. Among the rows of one device (aligned blocks of 96 rows) no expert is named by more than 42 rows, and in every draw some expert is named by exactly 42 rows of some device. `backward_routes`: each row names 6 different experts. Among the rows of one device (aligned blocks of 48 rows) no expert is named by more than 20 rows, and in every draw some expert is named by exactly 20 rows of some device.
All inputs are finite; a program needn't handle non-finite values.
Results may differ from the reference program's by a relative error of at most 0.0055.
Values may be sent and summed in bfloat16 or wider, within the bound.
A program may use at most 64 MiB of HBM per device.

```python
import math
import jax
import jax.numpy as jnp
import numpy as np
from jax import lax

D = 1024
HIDDEN_SIZE = 1024
TOPK = 6
TOK_DEV = 96
HALF = 512
BACK_DEV = 48
EXPERTS = 16
CAP_F = 42
CAP_B = 20
TOKENS_F = 3072
TOKENS_B = 1536
N_SECTION = 1
N_EXPERT = 32


def level_of(stream_key, extent, shards, least, largest):
    loudness = 1.0
    for position, parts in shards:
        steps = jax.random.uniform(jax.random.fold_in(jax.random.fold_in(stream_key, 6), position), (parts,), jnp.float32, least / len(shards), largest / len(shards))
        loudness = loudness * jnp.repeat(jnp.exp(steps), extent[position] // parts).reshape((-1,) + (1,) * (len(extent) - 1 - position))
    return loudness


def routed_block(rng, own, number, rows, number_of, top, limit, slope):
    order = jax.random.permutation(rng, number_of)
    crowded, ordinary = load_shares(number_of, rows * top, limit, slope, True), load_shares(number_of, rows * top, limit, slope, False)
    places = jnp.arange(number_of)

    def named(tallies, rotation):
        used = int((tallies > 0).sum())
        fixed = max(1, used // 4)
        shifted = fixed + (places - fixed + rotation * (used - fixed)) % max(1, number_of - fixed)
        return jnp.zeros((number_of,), jnp.int32).at[order[jnp.where(places < fixed, places, shifted)]].set(jnp.asarray(tallies, jnp.int32))

    tallies = jnp.where(number % 4 == 0, named(crowded, number // 4), named(ordinary, number - number // 4 - 1))
    mixed = jax.random.permutation(jax.random.fold_in(own, 3), number_of)
    source_of, sink = mixed[0:number_of // 2 * 2:2], mixed[1:number_of // 2 * 2:2]
    slack = jnp.minimum(tallies[source_of] - 1, limit - tallies[sink]) // 2
    slack = jnp.where((source_of == order[0]) | (sink == order[0]) | (tallies[sink] == 0), 0, jnp.maximum(slack, 0))
    shifted = jax.random.randint(jax.random.fold_in(own, 4), (number_of // 2,), 0, 1 << 20) % (slack + 1)
    tallies = tallies.at[source_of].add(-shifted).at[sink].add(shifted)
    items = jnp.searchsorted(jnp.cumsum(tallies), jnp.arange(rows * top), side="right").astype(jnp.int32)
    table = items.reshape(top, rows).T
    table = table[jax.random.permutation(jax.random.fold_in(own, 1), rows)]
    rotation = jax.random.randint(jax.random.fold_in(own, 2), (rows, 1), 0, top)
    return jnp.take_along_axis(table, (jnp.arange(top)[None, :] + rotation) % top, axis=1)


def load_shares(number_of, total, bound, slope, full):
    loads = [(1 << 20) // math.isqrt(standing ** slope) + 1 for standing in range(1, number_of + 1)]
    largest = bound if full else min(bound, max(-(-total // number_of), total * loads[0] // sum(loads)))
    least = 1 if total - largest >= number_of - 1 else 0
    given, spare = [largest] + [least] * (number_of - 1), total - largest - least * (number_of - 1)
    while spare > 0:
        candidates = [i for i in range(1, number_of) if given[i] < largest] or [i for i in range(1, number_of) if given[i] < bound]
        whole, left = sum([loads[i] for i in candidates]), spare
        for i in candidates:
            extra = min(bound - given[i], max(1, left * loads[i] // whole), spare)
            given[i] = given[i] + extra
            spare = spare - extra
    return np.array(given)


def bell_draw(own_key, extent, spread, limit, split=(), kind=jnp.bfloat16):
    gain = level_of(own_key, extent, split, -0.22, 0.18) if split else 1.0
    drawn = jax.random.normal(own_key, extent, jnp.float32) * spread * gain
    return jnp.minimum(jnp.maximum(drawn, -limit), limit).astype(kind)


def setup_inputs(seed: int = 0) -> dict:
    streams_of = jax.random.split(jax.random.key(seed), 10)
    forward_input = bell_draw(streams_of[0], (N_SECTION, TOKENS_F, D), 1.0, 6.0, ((1, 32),))
    forward_routes_keys = jax.random.split(jax.random.fold_in(streams_of[1], 1), N_SECTION * TOKENS_F // TOK_DEV)
    forward_routes_turns = jax.random.permutation(jax.random.fold_in(streams_of[1], 3), N_SECTION * TOKENS_F // TOK_DEV)
    forward_routes = jax.vmap(lambda own, number: routed_block(jax.random.fold_in(streams_of[1], 2), own, number, TOK_DEV, EXPERTS, TOPK, CAP_F, 2))(forward_routes_keys, forward_routes_turns).reshape((N_SECTION, TOKENS_F, TOPK))
    forward_gates = jnp.clip(0.05 + 0.55 * jax.random.uniform(streams_of[2], (N_SECTION, TOKENS_F, TOPK), jnp.float32) ** level_of(streams_of[2], (N_SECTION, TOKENS_F, TOPK), ((1, 32),), -0.2, 0.2), 0.05, 0.6)
    backward_input = bell_draw(streams_of[3], (N_SECTION, TOKENS_B, D), 1.0, 6.0, ((1, 32),))
    backward_routes_keys = jax.random.split(jax.random.fold_in(streams_of[4], 1), N_SECTION * TOKENS_B // BACK_DEV)
    backward_routes_turns = jax.random.permutation(jax.random.fold_in(streams_of[4], 3), N_SECTION * TOKENS_B // BACK_DEV)
    backward_routes = jax.vmap(lambda own, number: routed_block(jax.random.fold_in(streams_of[4], 2), own, number, BACK_DEV, EXPERTS, TOPK, CAP_B, 2))(backward_routes_keys, backward_routes_turns).reshape((N_SECTION, TOKENS_B, TOPK))
    backward_gates = jnp.clip(0.05 + 0.55 * jax.random.uniform(streams_of[5], (N_SECTION, TOKENS_B, TOPK), jnp.float32) ** level_of(streams_of[5], (N_SECTION, TOKENS_B, TOPK), ((1, 32),), -0.2, 0.2), 0.05, 0.6)
    output_grad = bell_draw(streams_of[6], (N_SECTION, TOKENS_B, D), 1.0, 6.0, ((1, 32),))
    weight_in = bell_draw(streams_of[7], (N_SECTION, N_EXPERT, D, 2 * HALF), D ** -0.5, 0.1875, ((1, 32),))
    weight_down = bell_draw(streams_of[8], (N_SECTION, N_EXPERT, HALF, D), HIDDEN_SIZE ** -0.5, 0.1875, ((1, 32),))
    return {"forward_input": forward_input, "forward_routes": forward_routes, "forward_gates": forward_gates, "backward_input": backward_input, "backward_routes": backward_routes, "backward_gates": backward_gates, "output_grad": output_grad, "weight_in": weight_in, "weight_down": weight_down}


def half_forward(token_rows, matrix_in, matrix_down):
    hidden = jnp.dot(token_rows, matrix_in, preferred_element_type=jnp.float32)
    half_width = matrix_down.shape[0]
    active = (jax.nn.silu(hidden[:, :half_width]) * hidden[:, half_width:]).astype(jnp.bfloat16)
    return jnp.dot(active, matrix_down, preferred_element_type=jnp.float32).astype(jnp.bfloat16)


def half_backward(token_rows, cotangent, matrix_in, matrix_down):
    hidden = jnp.dot(token_rows, matrix_in, preferred_element_type=jnp.float32)
    half_width = matrix_down.shape[0]
    gate_part = hidden[:, :half_width]
    up_part = hidden[:, half_width:]
    upstream = lax.dot_general(cotangent, matrix_down, (((1,), (1,)), ((), ())), preferred_element_type=jnp.float32)
    sigmoid_gate = jax.nn.sigmoid(gate_part)
    hidden_grad = jnp.concatenate(
        [upstream * up_part * sigmoid_gate * (1.0 + gate_part * (1.0 - sigmoid_gate)),
         upstream * gate_part * sigmoid_gate], axis=1).astype(jnp.bfloat16)
    return lax.dot_general(hidden_grad, matrix_in, (((1,), (1,)), ((), ())), preferred_element_type=jnp.float32).astype(jnp.bfloat16)


def slot_places(routes, block_rows, capacity):
    top_count = routes.shape[1]
    blocks = routes.reshape(-1, block_rows * top_count)
    expert_ids = jnp.arange(EXPERTS, dtype=jnp.int32)
    onehot = (blocks[:, :, None] == expert_ids[None, None, :]).astype(jnp.int32)
    earlier = jnp.cumsum(onehot, axis=1) - onehot
    placed = jnp.sum(earlier * onehot, axis=2)
    block_ids = jnp.arange(blocks.shape[0], dtype=jnp.int32)[:, None]
    return blocks.reshape(-1), (block_ids * capacity + placed).reshape(-1).astype(jnp.int32)


def mix_back(residual, gate_values, picked):
    mixed_out = residual.astype(jnp.float32) + jnp.sum(gate_values[:, :, None] * picked.astype(jnp.float32), axis=1)
    return mixed_out.astype(jnp.bfloat16)


def section_forward(tokens, routes, gate_values, weight_in, weight_down):
    token_count = tokens.shape[0]
    experts_of, slot_rows = slot_places(routes, TOK_DEV, CAP_F)
    owners = jnp.arange(token_count * TOPK, dtype=jnp.int32) // TOPK
    buffers = jnp.zeros((EXPERTS, N_EXPERT * CAP_F, D), tokens.dtype).at[experts_of, slot_rows].set(tokens[owners])
    pairs_in = weight_in.reshape(EXPERTS, 2, D, 2 * HALF)
    pairs_down = weight_down.reshape(EXPERTS, 2, HALF, D)

    def expert_run(operands):
        buffer, pair_in, pair_down = operands
        left_half = half_forward(buffer, pair_in[0], pair_down[0])
        right_half = half_forward(buffer, pair_in[1], pair_down[1])
        return (left_half.astype(jnp.float32) + right_half.astype(jnp.float32)).astype(jnp.bfloat16)

    outputs = lax.map(expert_run, (buffers, pairs_in, pairs_down))
    picked = outputs[experts_of, slot_rows].reshape(token_count, TOPK, D)
    return mix_back(tokens, gate_values, picked)


def section_backward(tokens, cotangent, routes, gate_values, weight_in, weight_down):
    token_count = tokens.shape[0]
    experts_of, slot_rows = slot_places(routes, BACK_DEV, CAP_B)
    owners = jnp.arange(token_count * TOPK, dtype=jnp.int32) // TOPK
    joined = jnp.concatenate([tokens, cotangent], axis=1)
    buffers = jnp.zeros((EXPERTS, N_EXPERT * CAP_B, 2 * D), tokens.dtype).at[experts_of, slot_rows].set(joined[owners])
    pairs_in = weight_in.reshape(EXPERTS, 2, D, 2 * HALF)
    pairs_down = weight_down.reshape(EXPERTS, 2, HALF, D)

    def expert_run(operands):
        buffer, pair_in, pair_down = operands
        left_half = half_backward(buffer[:, :D], buffer[:, D:], pair_in[0], pair_down[0])
        right_half = half_backward(buffer[:, :D], buffer[:, D:], pair_in[1], pair_down[1])
        return (left_half.astype(jnp.float32) + right_half.astype(jnp.float32)).astype(jnp.bfloat16)

    outputs = lax.map(expert_run, (buffers, pairs_in, pairs_down))
    picked = outputs[experts_of, slot_rows].reshape(token_count, TOPK, D)
    return mix_back(cotangent, gate_values, picked)


def reference(forward_input, forward_routes, forward_gates, backward_input, backward_routes, backward_gates, output_grad, weight_in, weight_down):
    forward_list = []
    backward_list = []
    for section_id in range(N_SECTION):
        forward_list.append(section_forward(forward_input[section_id], forward_routes[section_id], forward_gates[section_id],
                                          weight_in[section_id], weight_down[section_id]))
        backward_list.append(section_backward(backward_input[section_id], output_grad[section_id], backward_routes[section_id],
                                            backward_gates[section_id], weight_in[section_id], weight_down[section_id]))
    forward_sent = jnp.roll(jnp.stack(forward_list), 1, axis=0)
    backward_sent = jnp.roll(jnp.stack(backward_list), -1, axis=0)
    return forward_sent, backward_sent
```

```python
import functools
import jax
import jax.numpy as jnp
from jax import lax
from jax.experimental import pallas as pl
from jax.experimental.pallas import tpu as pltpu
from jax.sharding import PartitionSpec as P

PLANE = 4
NONE = -512.0
BF = jnp.bfloat16
F32 = jnp.float32
MESH = pl.DeviceIdType.MESH


def up16(count):
    return -(-count // 16) * 16


def dot(a, b):
    return jnp.dot(a, b, preferred_element_type=F32)


def dot_t(a, b):
    return lax.dot_general(a, b, (((1,), (1,)), ((), ())), preferred_element_type=F32)


def t_dot(a, b):
    return lax.dot_general(a, b, (((0,), (0,)), ((), ())), preferred_element_type=F32)


def iota(shape, dim):
    return lax.broadcasted_iota(jnp.int32, shape, dim)


def kernel(
    depth, experts, cap_f, cap_b,
    routes, gates, tok_f, tok_b, grad_b, w_in, w_down,
    out_f, out_b,
    blocks, send_d, recv_d, send_r, recv_r, send_p, recv_p, mine, acc_f, acc_b, own_f, own_b, wi, wd,
    sem_load, sem_ws, sem_wr, sem_gs, sem_gr, sem_ds, sem_dr, sem_rs, sem_rr, sem_ps, sem_pr,
):
    nf, width = tok_f.shape
    nb = tok_b.shape[0]
    half = w_down.shape[0]
    rf = up16(cap_f)
    rp = up16(2 * cap_b)
    rb = up16(cap_b)
    sec = lax.axis_index("section")
    me = lax.axis_index("expert")
    c = me % 2
    p = (me // 2) % PLANE
    z = me // (2 * PLANE)

    def dev(zz, pp, cc):
        return (sec, (zz * PLANE + pp) * 2 + cc)

    row_b, row_g, row_f = experts, experts + nb, experts + 2 * nb
    loads = [
        pltpu.make_async_copy(tok_b, blocks.at[z, pl.ds(row_b, nb)], sem_load.at[0]),
        pltpu.make_async_copy(grad_b, blocks.at[z, pl.ds(row_g, nb)], sem_load.at[1]),
        pltpu.make_async_copy(tok_f, blocks.at[z, pl.ds(row_f, nf)], sem_load.at[2]),
        pltpu.make_async_copy(w_in, wi.at[c], sem_load.at[3]),
        pltpu.make_async_copy(w_down, wd.at[c], sem_load.at[4]),
    ]
    for load in loads:
        load.start()

    barrier = pltpu.get_barrier_semaphore()
    pl.semaphore_signal(barrier, inc=1, device_id=dev(z, p, 1 - c), device_id_type=MESH)
    for q in range(1, PLANE):
        pl.semaphore_signal(
            barrier, inc=1, device_id=dev(z, (p + q) % PLANE, c), device_id_type=MESH
        )
    for q in range(1, depth):
        pl.semaphore_signal(
            barrier, inc=1, device_id=dev((z + q) % depth, p, c), device_id_type=MESH
        )

    lanes = routes.shape[1]
    e_ids = iota((experts, lanes), 0)
    named = jnp.zeros((experts, lanes), F32)
    weight = jnp.zeros((experts, lanes), F32)
    for k in range(routes.shape[0]):
        hit = routes[k : k + 1, :] == e_ids
        named = named + jnp.where(hit, 1.0, 0.0)
        weight = weight + jnp.where(hit, gates[k : k + 1, :], 0.0)
    first, second = iota((lanes, lanes), 0), iota((lanes, lanes), 1)
    earlier = jnp.where((first < second) & (first // 128 == second // 128), 1.0, 0.0).astype(BF)
    rank = dot(named.astype(BF), earlier)
    high = weight.astype(BF)
    low = (weight - high.astype(F32)).astype(BF)
    code = jnp.where(named > 0.0, rank, NONE).astype(BF)
    blocks[z, 0:experts, :] = jnp.concatenate(
        [code, high, low, jnp.zeros((experts, width - 3 * lanes), BF)], axis=1
    )

    pl.semaphore_wait(barrier, 1 + (PLANE - 1) + (depth - 1))

    weight_copies = [
        pltpu.make_async_remote_copy(
            w_in, wi.at[c], sem_ws.at[0], sem_wr.at[0], device_id=dev(z, p, 1 - c), device_id_type=MESH
        ),
        pltpu.make_async_remote_copy(
            w_down, wd.at[c], sem_ws.at[1], sem_wr.at[1], device_id=dev(z, p, 1 - c), device_id_type=MESH
        ),
    ]
    for load in loads[:3]:
        load.wait()

    def source(k):
        near = jnp.minimum(z, depth - 1 - z)
        side = jnp.where(k % 2 == 1, z - (k + 1) // 2, z + k // 2)
        far = jnp.where(2 * z < depth, k, depth - 1 - k)
        return jnp.where(k <= 2 * near, side, far)

    def relay(zs, way):
        return pltpu.make_async_remote_copy(
            blocks.at[zs], blocks.at[zs], sem_gs.at[zs, way], sem_gr.at[zs],
            device_id=dev((z + 1 if way else z + depth - 1) % depth, p, c), device_id_type=MESH,
        )

    def goes_right(zs):
        return (zs <= z) & (z < depth - 1)

    def goes_left(zs):
        return (zs >= z) & (z > 0)

    def send_on(zs):
        @pl.when(goes_right(zs))
        def _():
            relay(zs, 1).start()

        @pl.when(goes_left(zs))
        def _():
            relay(zs, 0).start()

    def dispatch_copy(zs, q):
        tgt = (p + q) % PLANE
        return pltpu.make_async_remote_copy(
            send_d.at[zs, tgt], recv_d.at[zs, p], sem_ds.at[zs, q], sem_dr.at[zs, p],
            device_id=dev(z, tgt, c), device_id_type=MESH,
        )

    def dispatch_arrival(zs, q):
        other = (p + q) % PLANE
        return pltpu.make_async_remote_copy(
            send_d.at[zs, other], recv_d.at[zs, other], sem_ds.at[zs, q], sem_dr.at[zs, other],
            device_id=dev(z, other, c), device_id_type=MESH,
        )

    def return_copy(zs, q):
        tgt = (p + q) % PLANE
        return pltpu.make_async_remote_copy(
            send_r.at[zs, tgt], recv_r.at[zs, p], sem_rs.at[zs, q], sem_rr.at[zs, p],
            device_id=dev(z, tgt, c), device_id_type=MESH,
        )

    def return_arrival(zs, q):
        other = (p + q) % PLANE
        return pltpu.make_async_remote_copy(
            send_r.at[zs, other], recv_r.at[zs, other], sem_rs.at[zs, q], sem_rr.at[zs, other],
            device_id=dev(z, other, c), device_id_type=MESH,
        )

    def part_copy(zs):
        return pltpu.make_async_remote_copy(
            send_p.at[zs], recv_p.at[z], sem_ps.at[zs], sem_pr.at[z],
            device_id=dev(zs, p, c), device_id_type=MESH,
        )

    def part_arrival(zs):
        return pltpu.make_async_remote_copy(
            send_p.at[zs], recv_p.at[zs], sem_ps.at[zs], sem_pr.at[zs],
            device_id=dev(zs, p, c), device_id_type=MESH,
        )

    def spread(zs, rows):
        total = PLANE * rows
        pick = jnp.where(
            iota((total, experts), 1) == z * PLANE + iota((total, experts), 0) // rows, 1.0, 0.0
        ).astype(BF)
        return dot(pick, blocks[zs, 0:experts, 0 : 3 * lanes])

    def slot(total, rows, count):
        return (iota((total, count), 0) % rows).astype(F32)

    def select(zs):
        table_f = spread(zs, rf)[:, 0:nf]
        pick_f = jnp.where(table_f == slot(PLANE * rf, rf, nf), 1.0, 0.0).astype(BF)
        rows_f = dot(pick_f, blocks[zs, row_f : row_f + nf, :]).astype(BF)
        table_b = spread(zs, rp)[:, 128 : 128 + nb]
        place = slot(PLANE * rp, rp, nb)
        pick_x = jnp.where(table_b == place, 1.0, 0.0).astype(BF)
        pick_g = jnp.where(table_b + cap_b == place, 1.0, 0.0).astype(BF)
        rows_b = (
            dot(pick_x, blocks[zs, row_b : row_b + nb, :])
            + dot(pick_g, blocks[zs, row_g : row_g + nb, :])
        ).astype(BF)
        for q in range(PLANE):
            send_d[zs, q, 0:rf, :] = rows_f[q * rf : (q + 1) * rf]
            send_d[zs, q, rf : rf + rp, :] = rows_b[q * rp : (q + 1) * rp]
        for q in range(1, PLANE):
            dispatch_copy(zs, q).start()
        recv_d[zs, p] = send_d[zs, p]

    def expert(zs):
        for q in range(1, PLANE):
            dispatch_arrival(zs, q).wait_recv()
        got = recv_d[zs]
        rows_f = got[:, 0:rf, :].reshape(PLANE * rf, width)
        rows_b = got[:, rf : rf + rp, :].reshape(PLANE * rp, width)
        shape = (PLANE * rb, PLANE * rp)
        row, col = iota(shape, 0), iota(shape, 1)
        same = (row // rb == col // rp) & (row % rb < cap_b)
        rows_x = dot(jnp.where(same & (col % rp == row % rb), 1.0, 0.0).astype(BF), rows_b)
        rows_g = dot(jnp.where(same & (col % rp == row % rb + cap_b), 1.0, 0.0).astype(BF), rows_b)
        mf, mb = PLANE * rf, PLANE * rb
        mine[0:mf] = rows_f
        mine[mf : mf + mb] = rows_x.astype(BF)
        mine[mf + mb : mf + 2 * mb] = rows_g.astype(BF)

        def one_half(h, carry):
            hidden = dot(mine[0 : mf + mb], wi[h])
            a, b = hidden[:, :half], hidden[:, half:]
            q = jax.nn.sigmoid(a)
            active = (a[:mf] * q[:mf] * b[:mf]).astype(BF)
            part_f = dot(active, wd[h])
            u = dot_t(mine[mf + mb : mf + 2 * mb], wd[h])
            a, b, q = a[mf:], b[mf:], q[mf:]
            grad = jnp.concatenate([u * b * q * (1.0 + a * (1.0 - q)), u * a * q], axis=1)
            part_b = dot_t(grad.astype(BF), wi[h])

            @pl.when(h == 0)
            def _():
                acc_f[...] = part_f
                acc_b[...] = part_b

            @pl.when(h == 1)
            def _():
                total_f = (acc_f[...] + part_f).astype(BF)
                total_b = (acc_b[...] + part_b).astype(BF)
                for j in range(PLANE):
                    send_r[zs, j, 0:rf, :] = total_f[j * rf : (j + 1) * rf]
                    send_r[zs, j, rf : rf + rb, :] = total_b[j * rb : (j + 1) * rb]

            return carry

        lax.fori_loop(0, 2, one_half, 0)
        for q in range(1, PLANE):
            return_copy(zs, q).start()
        recv_r[zs, p] = send_r[zs, p]

    def weigh(table, place, rows, count, lane):
        hit = table[:, lane : lane + count] == place
        high_part = jnp.where(hit, table[:, lanes + lane : lanes + lane + count], 0.0)
        low_part = jnp.where(hit, table[:, 2 * lanes + lane : 2 * lanes + lane + count], 0.0)
        return t_dot(high_part.astype(BF), rows) + t_dot(low_part.astype(BF), rows)

    def combine(zs):
        for q in range(1, PLANE):
            return_arrival(zs, q).wait_recv()
        got = recv_r[zs]
        rows_f = got[:, 0:rf, :].reshape(PLANE * rf, width)
        rows_b = got[:, rf : rf + rb, :].reshape(PLANE * rb, width)
        part_f = weigh(spread(zs, rf), slot(PLANE * rf, rf, nf), rows_f, nf, 0)
        part_b = weigh(spread(zs, rb), slot(PLANE * rb, rb, nb), rows_b, nb, 128)

        @pl.when(zs == z)
        def _():
            own_f[...] = part_f
            own_b[...] = part_b

        @pl.when(zs != z)
        def _():
            send_p[zs, 0:nf, :] = part_f.astype(BF)
            send_p[zs, nf : nf + nb, :] = part_b.astype(BF)
            part_copy(zs).start()

    def step(k, carry):
        @pl.when(k < depth)
        def _():
            zs = source(k)

            @pl.when(zs != z)
            def _():
                relay(zs, 0).wait_recv()

            send_on(zs)

            @pl.when(k == 0)
            def _():
                for copy in weight_copies:
                    copy.start()

            select(zs)

        @pl.when((k >= 1) & (k <= depth))
        def _():
            @pl.when(k == 1)
            def _():
                for load in loads[3:]:
                    load.wait()
                for copy in weight_copies:
                    copy.wait_recv()

            expert(source(k - 1))

        @pl.when(k >= 2)
        def _():
            combine(source(k - 2))

        return carry

    lax.fori_loop(0, depth + 2, step, 0)

    total_f = blocks[z, row_f : row_f + nf, :].astype(F32)
    total_b = blocks[z, row_g : row_g + nb, :].astype(F32)
    for q in range(1, depth):
        zs = (z + q) % depth
        part_arrival(zs).wait_recv()
        total_f = total_f + recv_p[zs, 0:nf, :].astype(F32)
        total_b = total_b + recv_p[zs, nf : nf + nb, :].astype(F32)
    out_f[...] = (total_f + own_f[...]).astype(BF)
    out_b[...] = (total_b + own_b[...]).astype(BF)

    for copy in weight_copies:
        copy.wait_send()

    def drain(zs, carry):
        @pl.when(goes_right(zs))
        def _():
            relay(zs, 1).wait_send()

        @pl.when(goes_left(zs))
        def _():
            relay(zs, 0).wait_send()

        for q in range(1, PLANE):
            dispatch_copy(zs, q).wait_send()
            return_copy(zs, q).wait_send()

        @pl.when(zs != z)
        def _():
            part_copy(zs).wait_send()

        return carry

    lax.fori_loop(0, depth, drain, 0)


def passed_along(block, axis, distance):
    count = lax.axis_size(axis)
    if count == 1:
        return block
    route = [((i - distance) % count, i) for i in range(count)]
    return lax.ppermute(block, axis, route)


def side_by_side(ahead, back, fill):
    def padded(array):
        return jnp.pad(array.T, ((0, 0), (0, 128 - array.shape[0])), constant_values=fill)

    return jnp.concatenate([padded(ahead), padded(back)], axis=1)


def on_device(
    forward_input, forward_routes, forward_gates,
    backward_input, backward_routes, backward_gates,
    output_grad, weight_in, weight_down,
):
    devices = lax.axis_size("expert")
    experts = devices // 2
    depth = experts // PLANE
    nf, width = forward_input.shape[1:]
    nb = backward_input.shape[1]
    half = weight_down.shape[2]
    cap_f = 2 * (7 * nf // (2 * experts))
    cap_b = 2 * (7 * nb // (2 * experts))
    rf, rp, rb = up16(cap_f), up16(2 * cap_b), up16(cap_b)
    routes = side_by_side(forward_routes[0], backward_routes[0], -1)
    gates = side_by_side(forward_gates[0], backward_gates[0], 0.0)
    vmem = pl.BlockSpec(memory_space=pltpu.VMEM)
    anywhere = pl.BlockSpec(memory_space=pl.ANY)
    dma = pltpu.SemaphoreType.DMA
    ahead, back = pl.pallas_call(
        functools.partial(kernel, depth, experts, cap_f, cap_b),
        out_shape=(
            jax.ShapeDtypeStruct((nf, width), BF),
            jax.ShapeDtypeStruct((nb, width), BF),
        ),
        in_specs=[vmem] * 2 + [anywhere] * 5,
        out_specs=(vmem, vmem),
        scratch_shapes=[
            pltpu.VMEM((depth, experts + 2 * nb + nf, width), BF),
            pltpu.VMEM((depth, PLANE, rf + rp, width), BF),
            pltpu.VMEM((depth, PLANE, rf + rp, width), BF),
            pltpu.VMEM((depth, PLANE, rf + rb, width), BF),
            pltpu.VMEM((depth, PLANE, rf + rb, width), BF),
            pltpu.VMEM((depth, nf + nb, width), BF),
            pltpu.VMEM((depth, nf + nb, width), BF),
            pltpu.VMEM((PLANE * (rf + 2 * rb), width), BF),
            pltpu.VMEM((PLANE * rf, width), F32),
            pltpu.VMEM((PLANE * rb, width), F32),
            pltpu.VMEM((nf, width), F32),
            pltpu.VMEM((nb, width), F32),
            pltpu.VMEM((2, width, 2 * half), BF),
            pltpu.VMEM((2, half, width), BF),
            dma((5,)),
            dma((2,)),
            dma((2,)),
            dma((depth, 2)),
            dma((depth,)),
            dma((depth, PLANE)),
            dma((depth, PLANE)),
            dma((depth, PLANE)),
            dma((depth, PLANE)),
            dma((depth,)),
            dma((depth,)),
        ],
        compiler_params=pltpu.CompilerParams(
            collective_id=0, has_side_effects=True, vmem_limit_bytes=56 * 1024 * 1024
        ),
    )(
        routes, gates, forward_input[0], backward_input[0], output_grad[0],
        weight_in[0, 0], weight_down[0, 0],
    )
    forward_sent = passed_along(ahead[None], "section", 1)
    backward_sent = passed_along(back[None], "section", -1)
    return (forward_sent, backward_sent)


def solution(mesh):
    rows = P("section", "expert", None)
    weights = P("section", "expert", None, None)
    return jax.shard_map(
        on_device,
        mesh=mesh,
        in_specs=(rows,) * 7 + (weights,) * 2,
        out_specs=(rows, rows),
        check_vma=False,
    )
```

```python
import functools
import jax
import jax.numpy as jnp
from jax import lax
from jax.experimental import pallas as pl
from jax.experimental.pallas import tpu as pltpu
from jax.sharding import PartitionSpec as P

PLANE = 4
NONE = -512.0
BF = jnp.bfloat16
F32 = jnp.float32
MESH = pl.DeviceIdType.MESH


def up16(count):
    return -(-count // 16) * 16


def dot(a, b):
    return jnp.dot(a, b, preferred_element_type=F32)


def dot_t(a, b):
    return lax.dot_general(a, b, (((1,), (1,)), ((), ())), preferred_element_type=F32)


def t_dot(a, b):
    return lax.dot_general(a, b, (((0,), (0,)), ((), ())), preferred_element_type=F32)


def iota(shape, dim):
    return lax.broadcasted_iota(jnp.int32, shape, dim)


def kernel(
    depth, experts, cap_f, cap_b,
    routes_f, gates_f, routes_b, gates_b, tok_f, tok_b, grad_b, w_in, w_down,
    out_f, out_b,
    blocks, send_d, recv_d, send_r, recv_r, send_p, recv_p, mine, acc_f, acc_b, own_f, own_b, wi, wd,
    sem_load, sem_ws, sem_wr, sem_gs, sem_gr, sem_ds, sem_dr, sem_rs, sem_rr, sem_ps, sem_pr,
):
    nf, width = tok_f.shape
    nb = tok_b.shape[0]
    half = w_down.shape[0]
    rf = up16(cap_f)
    rp = up16(2 * cap_b)
    rb = up16(cap_b)
    rr = up16(cap_f + cap_b)
    sec = lax.axis_index("section")
    me = lax.axis_index("expert")
    c = me % 2
    p = (me // 2) % PLANE
    z = me // (2 * PLANE)

    def dev(zz, pp, cc):
        return (sec, (zz * PLANE + pp) * 2 + cc)

    row_b, row_g, row_f = experts, experts + nb, experts + 2 * nb
    loads = [
        pltpu.make_async_copy(tok_b, blocks.at[z, pl.ds(row_b, nb)], sem_load.at[0]),
        pltpu.make_async_copy(grad_b, blocks.at[z, pl.ds(row_g, nb)], sem_load.at[1]),
        pltpu.make_async_copy(tok_f, blocks.at[z, pl.ds(row_f, nf)], sem_load.at[2]),
        pltpu.make_async_copy(w_in, wi.at[c], sem_load.at[3]),
        pltpu.make_async_copy(w_down, wd.at[c], sem_load.at[4]),
    ]
    for load in loads:
        load.start()

    barrier = pltpu.get_barrier_semaphore()
    pl.semaphore_signal(barrier, inc=1, device_id=dev(z, p, 1 - c), device_id_type=MESH)
    for q in range(1, PLANE):
        pl.semaphore_signal(
            barrier, inc=1, device_id=dev(z, (p + q) % PLANE, c), device_id_type=MESH
        )
    for q in range(1, depth):
        pl.semaphore_signal(
            barrier, inc=1, device_id=dev((z + q) % depth, p, c), device_id_type=MESH
        )

    lanes = 256
    blocks[z, 0:experts, :] = jnp.zeros((experts, width), BF)
    for routes, gates, lane in ((routes_f, gates_f, 0), (routes_b, gates_b, 128)):
        count = routes.shape[2]
        e_ids = iota((experts, count), 0)
        named = jnp.zeros((experts, count), F32)
        weight = jnp.zeros((experts, count), F32)
        for k in range(routes.shape[0]):
            hit = routes[k] == e_ids
            named = named + jnp.where(hit, 1.0, 0.0)
            weight = weight + jnp.where(hit, gates[k], 0.0)
        earlier = jnp.where(iota((count, count), 0) < iota((count, count), 1), 1.0, 0.0)
        rank = dot(named.astype(BF), earlier.astype(BF))
        high = weight.astype(BF)
        low = (weight - high.astype(F32)).astype(BF)
        code = jnp.where(named > 0.0, rank, NONE).astype(BF)
        for part, values in enumerate((code, high, low)):
            start = part * lanes + lane
            blocks[z, 0:experts, start : start + count] = values

    pl.semaphore_wait(barrier, 1 + (PLANE - 1) + (depth - 1))

    weight_copies = [
        pltpu.make_async_remote_copy(
            w_in, wi.at[c], sem_ws.at[0], sem_wr.at[0], device_id=dev(z, p, 1 - c), device_id_type=MESH
        ),
        pltpu.make_async_remote_copy(
            w_down, wd.at[c], sem_ws.at[1], sem_wr.at[1], device_id=dev(z, p, 1 - c), device_id_type=MESH
        ),
    ]
    for load in loads[:3]:
        load.wait()

    def source(k):
        near = jnp.minimum(z, depth - 1 - z)
        side = jnp.where(k % 2 == 1, z - (k + 1) // 2, z + k // 2)
        far = jnp.where(2 * z < depth, k, depth - 1 - k)
        return jnp.where(k <= 2 * near, side, far)

    def relay(zs, way):
        return pltpu.make_async_remote_copy(
            blocks.at[zs], blocks.at[zs], sem_gs.at[zs, way], sem_gr.at[zs],
            device_id=dev((z + 1 if way else z + depth - 1) % depth, p, c), device_id_type=MESH,
        )

    def goes_right(zs):
        return (zs <= z) & (z < depth - 1)

    def goes_left(zs):
        return (zs >= z) & (z > 0)

    def send_on(zs):
        @pl.when(goes_right(zs))
        def _():
            relay(zs, 1).start()

        @pl.when(goes_left(zs))
        def _():
            relay(zs, 0).start()

    def dispatch_copy(zs, q):
        tgt = (p + q) % PLANE
        return pltpu.make_async_remote_copy(
            send_d.at[zs, tgt], recv_d.at[zs, p], sem_ds.at[zs, q], sem_dr.at[zs, p],
            device_id=dev(z, tgt, c), device_id_type=MESH,
        )

    def dispatch_arrival(zs, q):
        other = (p + q) % PLANE
        return pltpu.make_async_remote_copy(
            send_d.at[zs, other], recv_d.at[zs, other], sem_ds.at[zs, q], sem_dr.at[zs, other],
            device_id=dev(z, other, c), device_id_type=MESH,
        )

    def return_copy(zs, q):
        tgt = (p + q) % PLANE
        return pltpu.make_async_remote_copy(
            send_r.at[zs, tgt], recv_r.at[zs, p], sem_rs.at[zs, q], sem_rr.at[zs, p],
            device_id=dev(z, tgt, c), device_id_type=MESH,
        )

    def return_arrival(zs, q):
        other = (p + q) % PLANE
        return pltpu.make_async_remote_copy(
            send_r.at[zs, other], recv_r.at[zs, other], sem_rs.at[zs, q], sem_rr.at[zs, other],
            device_id=dev(z, other, c), device_id_type=MESH,
        )

    def part_copy(zs):
        return pltpu.make_async_remote_copy(
            send_p.at[zs], recv_p.at[z], sem_ps.at[zs], sem_pr.at[z],
            device_id=dev(zs, p, c), device_id_type=MESH,
        )

    def part_arrival(zs):
        return pltpu.make_async_remote_copy(
            send_p.at[zs], recv_p.at[zs], sem_ps.at[zs], sem_pr.at[zs],
            device_id=dev(zs, p, c), device_id_type=MESH,
        )

    def spread(zs, rows):
        total = PLANE * rows
        pick = jnp.where(
            iota((total, experts), 1) == z * PLANE + iota((total, experts), 0) // rows, 1.0, 0.0
        ).astype(BF)
        return dot(pick, blocks[zs, 0:experts, 0 : 3 * lanes])

    def slot(total, rows, count):
        return (iota((total, count), 0) % rows).astype(F32)

    def select(zs):
        table_f = spread(zs, rf)[:, 0:nf]
        pick_f = jnp.where(table_f == slot(PLANE * rf, rf, nf), 1.0, 0.0).astype(BF)
        rows_f = dot(pick_f, blocks[zs, row_f : row_f + nf, :]).astype(BF)
        table_b = spread(zs, rp)[:, 128 : 128 + nb]
        place = slot(PLANE * rp, rp, nb)
        pick_x = jnp.where(table_b == place, 1.0, 0.0).astype(BF)
        pick_g = jnp.where(table_b + cap_b == place, 1.0, 0.0).astype(BF)
        rows_b = (
            dot(pick_x, blocks[zs, row_b : row_b + nb, :])
            + dot(pick_g, blocks[zs, row_g : row_g + nb, :])
        ).astype(BF)
        for q in range(PLANE):
            send_d[zs, q, 0:rf, :] = rows_f[q * rf : (q + 1) * rf]
            send_d[zs, q, rf : rf + rp, :] = rows_b[q * rp : (q + 1) * rp]
        for q in range(1, PLANE):
            dispatch_copy(zs, q).start()
        recv_d[zs, p] = send_d[zs, p]

    def pack(rows, start, count):
        row, col = iota((PLANE * rr, PLANE * rows), 0), iota((PLANE * rr, PLANE * rows), 1)
        place = row % rr - start
        hit = (row // rr == col // rows) & (place == col % rows) & (place >= 0) & (place < count)
        return jnp.where(hit, 1.0, 0.0).astype(BF)

    def expert(zs):
        for q in range(1, PLANE):
            dispatch_arrival(zs, q).wait_recv()
        got = recv_d[zs]
        rows_f = got[:, 0:rf, :].reshape(PLANE * rf, width)
        rows_b = got[:, rf : rf + rp, :].reshape(PLANE * rp, width)
        shape = (PLANE * rb, PLANE * rp)
        row, col = iota(shape, 0), iota(shape, 1)
        same = (row // rb == col // rp) & (row % rb < cap_b)
        rows_x = dot(jnp.where(same & (col % rp == row % rb), 1.0, 0.0).astype(BF), rows_b)
        rows_g = dot(jnp.where(same & (col % rp == row % rb + cap_b), 1.0, 0.0).astype(BF), rows_b)
        mf, mb = PLANE * rf, PLANE * rb
        mine[0:mf] = rows_f
        mine[mf : mf + mb] = rows_x.astype(BF)
        mine[mf + mb : mf + 2 * mb] = rows_g.astype(BF)

        def one_half(h, carry):
            hidden = dot(mine[0 : mf + mb], wi[h])
            a, b = hidden[:, :half], hidden[:, half:]
            q = jax.nn.sigmoid(a)
            active = (a[:mf] * q[:mf] * b[:mf]).astype(BF)
            part_f = dot(active, wd[h])
            u = dot_t(mine[mf + mb : mf + 2 * mb], wd[h])
            a, b, q = a[mf:], b[mf:], q[mf:]
            grad = jnp.concatenate([u * b * q * (1.0 + a * (1.0 - q)), u * a * q], axis=1)
            part_b = dot_t(grad.astype(BF), wi[h])

            @pl.when(h == 0)
            def _():
                acc_f[...] = part_f
                acc_b[...] = part_b

            @pl.when(h == 1)
            def _():
                total_f = (acc_f[...] + part_f).astype(BF)
                total_b = (acc_b[...] + part_b).astype(BF)
                packed = dot(pack(rf, 0, cap_f), total_f) + dot(pack(rb, cap_f, cap_b), total_b)
                packed = packed.astype(BF)
                for j in range(PLANE):
                    send_r[zs, j] = packed[j * rr : (j + 1) * rr]

            return carry

        lax.fori_loop(0, 2, one_half, 0)
        for q in range(1, PLANE):
            return_copy(zs, q).start()
        recv_r[zs, p] = send_r[zs, p]

    def weigh(table, place, rows, count, lane):
        hit = table[:, lane : lane + count] == place
        high_part = jnp.where(hit, table[:, lanes + lane : lanes + lane + count], 0.0)
        low_part = jnp.where(hit, table[:, 2 * lanes + lane : 2 * lanes + lane + count], 0.0)
        return t_dot(high_part.astype(BF), rows) + t_dot(low_part.astype(BF), rows)

    def combine(zs):
        for q in range(1, PLANE):
            return_arrival(zs, q).wait_recv()
        rows = recv_r[zs].reshape(PLANE * rr, width)
        table = spread(zs, rr)
        part_f = weigh(table, slot(PLANE * rr, rr, nf), rows, nf, 0)
        part_b = weigh(table, slot(PLANE * rr, rr, nb) - cap_f, rows, nb, 128)

        @pl.when(zs == z)
        def _():
            own_f[...] = part_f
            own_b[...] = part_b

        @pl.when(zs != z)
        def _():
            send_p[zs, 0:nf, :] = part_f.astype(BF)
            send_p[zs, nf : nf + nb, :] = part_b.astype(BF)
            part_copy(zs).start()

    def step(k, carry):
        @pl.when(k < depth)
        def _():
            zs = source(k)

            @pl.when(zs != z)
            def _():
                relay(zs, 0).wait_recv()

            send_on(zs)

            @pl.when(k == 0)
            def _():
                for copy in weight_copies:
                    copy.start()

            select(zs)

        @pl.when((k >= 2) & (k <= depth + 1))
        def _():
            @pl.when(k == 2)
            def _():
                for load in loads[3:]:
                    load.wait()
                for copy in weight_copies:
                    copy.wait_recv()

            expert(source((k - 1) % depth))

        @pl.when(k >= 3)
        def _():
            combine(source((k - 2) % depth))

        return carry

    lax.fori_loop(0, depth + 3, step, 0)

    total_f = blocks[z, row_f : row_f + nf, :].astype(F32)
    total_b = blocks[z, row_g : row_g + nb, :].astype(F32)
    for q in range(1, depth):
        zs = (z + q) % depth
        part_arrival(zs).wait_recv()
        total_f = total_f + recv_p[zs, 0:nf, :].astype(F32)
        total_b = total_b + recv_p[zs, nf : nf + nb, :].astype(F32)
    out_f[...] = (total_f + own_f[...]).astype(BF)
    out_b[...] = (total_b + own_b[...]).astype(BF)

    for copy in weight_copies:
        copy.wait_send()

    def drain(zs, carry):
        @pl.when(goes_right(zs))
        def _():
            relay(zs, 1).wait_send()

        @pl.when(goes_left(zs))
        def _():
            relay(zs, 0).wait_send()

        for q in range(1, PLANE):
            dispatch_copy(zs, q).wait_send()
            return_copy(zs, q).wait_send()

        @pl.when(zs != z)
        def _():
            part_copy(zs).wait_send()

        return carry

    lax.fori_loop(0, depth, drain, 0)


def passed_along(block, axis, distance):
    count = lax.axis_size(axis)
    if count == 1:
        return block
    route = [((i - distance) % count, i) for i in range(count)]
    return lax.ppermute(block, axis, route)


def on_device(
    forward_input, forward_routes, forward_gates,
    backward_input, backward_routes, backward_gates,
    output_grad, weight_in, weight_down,
):
    devices = lax.axis_size("expert")
    experts = devices // 2
    depth = experts // PLANE
    nf, width = forward_input.shape[1:]
    nb = backward_input.shape[1]
    half = weight_down.shape[2]
    cap_f = 2 * (7 * nf // (2 * experts))
    cap_b = 2 * (7 * nb // (2 * experts))
    rf, rp, rb = up16(cap_f), up16(2 * cap_b), up16(cap_b)
    rr = up16(cap_f + cap_b)
    tables = [
        jnp.transpose(array, (2, 0, 1))
        for array in (forward_routes, forward_gates, backward_routes, backward_gates)
    ]
    vmem = pl.BlockSpec(memory_space=pltpu.VMEM)
    anywhere = pl.BlockSpec(memory_space=pl.ANY)
    dma = pltpu.SemaphoreType.DMA
    ahead, back = pl.pallas_call(
        functools.partial(kernel, depth, experts, cap_f, cap_b),
        out_shape=(
            jax.ShapeDtypeStruct((nf, width), BF),
            jax.ShapeDtypeStruct((nb, width), BF),
        ),
        in_specs=[vmem] * 4 + [anywhere] * 5,
        out_specs=(vmem, vmem),
        scratch_shapes=[
            pltpu.VMEM((depth, experts + 2 * nb + nf, width), BF),
            pltpu.VMEM((depth, PLANE, rf + rp, width), BF),
            pltpu.VMEM((depth, PLANE, rf + rp, width), BF),
            pltpu.VMEM((depth, PLANE, rr, width), BF),
            pltpu.VMEM((depth, PLANE, rr, width), BF),
            pltpu.VMEM((depth, nf + nb, width), BF),
            pltpu.VMEM((depth, nf + nb, width), BF),
            pltpu.VMEM((PLANE * (rf + 2 * rb), width), BF),
            pltpu.VMEM((PLANE * rf, width), F32),
            pltpu.VMEM((PLANE * rb, width), F32),
            pltpu.VMEM((nf, width), F32),
            pltpu.VMEM((nb, width), F32),
            pltpu.VMEM((2, width, 2 * half), BF),
            pltpu.VMEM((2, half, width), BF),
            dma((5,)),
            dma((2,)),
            dma((2,)),
            dma((depth, 2)),
            dma((depth,)),
            dma((depth, PLANE)),
            dma((depth, PLANE)),
            dma((depth, PLANE)),
            dma((depth, PLANE)),
            dma((depth,)),
            dma((depth,)),
        ],
        compiler_params=pltpu.CompilerParams(
            collective_id=0, has_side_effects=True, vmem_limit_bytes=56 * 1024 * 1024
        ),
    )(
        *tables, forward_input[0], backward_input[0], output_grad[0],
        weight_in[0, 0], weight_down[0, 0],
    )
    forward_sent = passed_along(ahead[None], "section", 1)
    backward_sent = passed_along(back[None], "section", -1)
    return (forward_sent, backward_sent)


def solution(mesh):
    rows = P("section", "expert", None)
    weights = P("section", "expert", None, None)
    return jax.shard_map(
        on_device,
        mesh=mesh,
        in_specs=(rows,) * 7 + (weights,) * 2,
        out_specs=(rows, rows),
        check_vma=False,
    )
```

```python
import functools
import jax
import jax.numpy as jnp
from jax import lax
from jax.experimental import pallas as pl
from jax.experimental.pallas import tpu as pltpu
from jax.sharding import PartitionSpec as P

PLANE = 4
NONE = -512.0
BF = jnp.bfloat16
F32 = jnp.float32
MESH = pl.DeviceIdType.MESH


def up16(count):
    return -(-count // 16) * 16


def dot(a, b):
    return jnp.dot(a, b, preferred_element_type=F32)


def dot_t(a, b):
    return lax.dot_general(a, b, (((1,), (1,)), ((), ())), preferred_element_type=F32)


def t_dot(a, b):
    return lax.dot_general(a, b, (((0,), (0,)), ((), ())), preferred_element_type=F32)


def iota(shape, dim):
    return lax.broadcasted_iota(jnp.int32, shape, dim)


def kernel(
    depth, experts, cap_f, cap_b,
    routes_f, gates_f, routes_b, gates_b, tok_f, tok_b, grad_b, w_in, w_down,
    out_f, out_b,
    blocks, send_d, recv_d, send_r, recv_r, send_p, recv_p, mine, acc_f, acc_b, own_f, own_b, wi, wd,
    sem_load, sem_ws, sem_wr, sem_gs, sem_gr, sem_ds, sem_dr, sem_rs, sem_rr, sem_ps, sem_pr,
):
    nf, width = tok_f.shape
    nb = tok_b.shape[0]
    half = w_down.shape[0]
    rf = up16(cap_f)
    rp = up16(2 * cap_b)
    rb = up16(cap_b)
    rr = up16(cap_f + cap_b)
    sec = lax.axis_index("section")
    me = lax.axis_index("expert")
    c = me % 2
    p = (me // 2) % PLANE
    z = me // (2 * PLANE)

    def dev(zz, pp, cc):
        return (sec, (zz * PLANE + pp) * 2 + cc)

    row_b, row_g, row_f = experts, experts + nb, experts + 2 * nb
    loads = [
        pltpu.make_async_copy(tok_b, blocks.at[z, pl.ds(row_b, nb)], sem_load.at[0]),
        pltpu.make_async_copy(grad_b, blocks.at[z, pl.ds(row_g, nb)], sem_load.at[1]),
        pltpu.make_async_copy(tok_f, blocks.at[z, pl.ds(row_f, nf)], sem_load.at[2]),
        pltpu.make_async_copy(w_in, wi.at[c], sem_load.at[3]),
        pltpu.make_async_copy(w_down, wd.at[c], sem_load.at[4]),
    ]
    for load in loads:
        load.start()

    barrier = pltpu.get_barrier_semaphore()
    pl.semaphore_signal(barrier, inc=1, device_id=dev(z, p, 1 - c), device_id_type=MESH)
    for q in range(1, PLANE):
        pl.semaphore_signal(
            barrier, inc=1, device_id=dev(z, (p + q) % PLANE, c), device_id_type=MESH
        )
    for q in range(1, depth):
        pl.semaphore_signal(
            barrier, inc=1, device_id=dev((z + q) % depth, p, c), device_id_type=MESH
        )

    lanes = 256
    blocks[z, 0:experts, :] = jnp.zeros((experts, width), BF)
    for routes, gates, lane in ((routes_f, gates_f, 0), (routes_b, gates_b, 128)):
        count = routes.shape[2]
        e_ids = iota((experts, count), 0)
        named = jnp.zeros((experts, count), F32)
        weight = jnp.zeros((experts, count), F32)
        for k in range(routes.shape[0]):
            hit = routes[k] == e_ids
            named = named + jnp.where(hit, 1.0, 0.0)
            weight = weight + jnp.where(hit, gates[k], 0.0)
        earlier = jnp.where(iota((count, count), 0) < iota((count, count), 1), 1.0, 0.0)
        rank = dot(named.astype(BF), earlier.astype(BF))
        high = weight.astype(BF)
        low = (weight - high.astype(F32)).astype(BF)
        code = jnp.where(named > 0.0, rank, NONE).astype(BF)
        for part, values in enumerate((code, high, low)):
            start = part * lanes + lane
            blocks[z, 0:experts, start : start + count] = values

    pl.semaphore_wait(barrier, 1 + (PLANE - 1) + (depth - 1))

    weight_copies = [
        pltpu.make_async_remote_copy(
            w_in, wi.at[c], sem_ws.at[0], sem_wr.at[0], device_id=dev(z, p, 1 - c), device_id_type=MESH
        ),
        pltpu.make_async_remote_copy(
            w_down, wd.at[c], sem_ws.at[1], sem_wr.at[1], device_id=dev(z, p, 1 - c), device_id_type=MESH
        ),
    ]
    for load in loads[:3]:
        load.wait()

    def source(k):
        near = jnp.minimum(z, depth - 1 - z)
        side = jnp.where(k % 2 == 1, z - (k + 1) // 2, z + k // 2)
        far = jnp.where(2 * z < depth, k, depth - 1 - k)
        return jnp.where(k <= 2 * near, side, far)

    def relay(zs, way):
        return pltpu.make_async_remote_copy(
            blocks.at[zs], blocks.at[zs], sem_gs.at[zs, way], sem_gr.at[zs],
            device_id=dev((z + 1 if way else z + depth - 1) % depth, p, c), device_id_type=MESH,
        )

    def goes_right(zs):
        return (zs <= z) & (z < depth - 1)

    def goes_left(zs):
        return (zs >= z) & (z > 0)

    def passes_through(zs):
        return (zs != z) & (goes_right(zs) | goes_left(zs))

    def send_on(zs):
        @pl.when(goes_right(zs))
        def _():
            relay(zs, 1).start()

        @pl.when(goes_left(zs))
        def _():
            relay(zs, 0).start()

    def dispatch_copy(zs, q):
        tgt = (p + q) % PLANE
        return pltpu.make_async_remote_copy(
            send_d.at[zs, tgt], recv_d.at[zs, p], sem_ds.at[zs, q], sem_dr.at[zs, p],
            device_id=dev(z, tgt, c), device_id_type=MESH,
        )

    def dispatch_arrival(zs, q):
        other = (p + q) % PLANE
        return pltpu.make_async_remote_copy(
            send_d.at[zs, other], recv_d.at[zs, other], sem_ds.at[zs, q], sem_dr.at[zs, other],
            device_id=dev(z, other, c), device_id_type=MESH,
        )

    def return_copy(zs, q):
        tgt = (p + q) % PLANE
        return pltpu.make_async_remote_copy(
            send_r.at[zs, tgt], recv_r.at[zs, p], sem_rs.at[zs, q], sem_rr.at[zs, p],
            device_id=dev(z, tgt, c), device_id_type=MESH,
        )

    def return_arrival(zs, q):
        other = (p + q) % PLANE
        return pltpu.make_async_remote_copy(
            send_r.at[zs, other], recv_r.at[zs, other], sem_rs.at[zs, q], sem_rr.at[zs, other],
            device_id=dev(z, other, c), device_id_type=MESH,
        )

    def part_copy(zs):
        return pltpu.make_async_remote_copy(
            send_p.at[zs], recv_p.at[z], sem_ps.at[zs], sem_pr.at[z],
            device_id=dev(zs, p, c), device_id_type=MESH,
        )

    def part_arrival(zs):
        return pltpu.make_async_remote_copy(
            send_p.at[zs], recv_p.at[zs], sem_ps.at[zs], sem_pr.at[zs],
            device_id=dev(zs, p, c), device_id_type=MESH,
        )

    def spread(zs, rows):
        total = PLANE * rows
        pick = jnp.where(
            iota((total, experts), 1) == z * PLANE + iota((total, experts), 0) // rows, 1.0, 0.0
        ).astype(BF)
        return dot(pick, blocks[zs, 0:experts, 0 : 3 * lanes])

    def slot(total, rows, count):
        return (iota((total, count), 0) % rows).astype(F32)

    def select(zs):
        table_f = spread(zs, rf)[:, 0:nf]
        pick_f = jnp.where(table_f == slot(PLANE * rf, rf, nf), 1.0, 0.0).astype(BF)
        rows_f = dot(pick_f, blocks[zs, row_f : row_f + nf, :]).astype(BF)
        table_b = spread(zs, rp)[:, 128 : 128 + nb]
        place = slot(PLANE * rp, rp, nb)
        pick_x = jnp.where(table_b == place, 1.0, 0.0).astype(BF)
        pick_g = jnp.where(table_b + cap_b == place, 1.0, 0.0).astype(BF)
        rows_b = (
            dot(pick_x, blocks[zs, row_b : row_b + nb, :])
            + dot(pick_g, blocks[zs, row_g : row_g + nb, :])
        ).astype(BF)
        for q in range(PLANE):
            send_d[zs, q, 0:rf, :] = rows_f[q * rf : (q + 1) * rf]
            send_d[zs, q, rf : rf + rp, :] = rows_b[q * rp : (q + 1) * rp]
        for q in range(1, PLANE):
            dispatch_copy(zs, q).start()
        recv_d[zs, p] = send_d[zs, p]

    def pack(rows, start, count):
        row, col = iota((PLANE * rr, PLANE * rows), 0), iota((PLANE * rr, PLANE * rows), 1)
        place = row % rr - start
        hit = (row // rr == col // rows) & (place == col % rows) & (place >= 0) & (place < count)
        return jnp.where(hit, 1.0, 0.0).astype(BF)

    def expert(zs):
        for q in range(1, PLANE):
            dispatch_arrival(zs, q).wait_recv()
        got = recv_d[zs]
        rows_f = got[:, 0:rf, :].reshape(PLANE * rf, width)
        rows_b = got[:, rf : rf + rp, :].reshape(PLANE * rp, width)
        shape = (PLANE * rb, PLANE * rp)
        row, col = iota(shape, 0), iota(shape, 1)
        same = (row // rb == col // rp) & (row % rb < cap_b)
        rows_x = dot(jnp.where(same & (col % rp == row % rb), 1.0, 0.0).astype(BF), rows_b)
        rows_g = dot(jnp.where(same & (col % rp == row % rb + cap_b), 1.0, 0.0).astype(BF), rows_b)
        mf, mb = PLANE * rf, PLANE * rb
        mine[0:mf] = rows_f
        mine[mf : mf + mb] = rows_x.astype(BF)
        mine[mf + mb : mf + 2 * mb] = rows_g.astype(BF)

        def one_half(h, carry):
            hidden = dot(mine[0 : mf + mb], wi[h])
            a, b = hidden[:, :half], hidden[:, half:]
            q = jax.nn.sigmoid(a)
            active = (a[:mf] * q[:mf] * b[:mf]).astype(BF)
            part_f = dot(active, wd[h])
            u = dot_t(mine[mf + mb : mf + 2 * mb], wd[h])
            a, b, q = a[mf:], b[mf:], q[mf:]
            grad = jnp.concatenate([u * b * q * (1.0 + a * (1.0 - q)), u * a * q], axis=1)
            part_b = dot_t(grad.astype(BF), wi[h])

            @pl.when(h == 0)
            def _():
                acc_f[...] = part_f
                acc_b[...] = part_b

            @pl.when(h == 1)
            def _():
                total_f = (acc_f[...] + part_f).astype(BF)
                total_b = (acc_b[...] + part_b).astype(BF)
                packed = dot(pack(rf, 0, cap_f), total_f) + dot(pack(rb, cap_f, cap_b), total_b)
                packed = packed.astype(BF)
                for j in range(PLANE):
                    send_r[zs, j] = packed[j * rr : (j + 1) * rr]

            return carry

        lax.fori_loop(0, 2, one_half, 0)
        for q in range(1, PLANE):
            return_copy(zs, q).start()
        recv_r[zs, p] = send_r[zs, p]

    def weigh(table, place, rows, count, lane):
        hit = table[:, lane : lane + count] == place
        high_part = jnp.where(hit, table[:, lanes + lane : lanes + lane + count], 0.0)
        low_part = jnp.where(hit, table[:, 2 * lanes + lane : 2 * lanes + lane + count], 0.0)
        return t_dot(high_part.astype(BF), rows) + t_dot(low_part.astype(BF), rows)

    def combine(zs):
        for q in range(1, PLANE):
            return_arrival(zs, q).wait_recv()
        rows = recv_r[zs].reshape(PLANE * rr, width)
        table = spread(zs, rr)
        part_f = weigh(table, slot(PLANE * rr, rr, nf), rows, nf, 0)
        part_b = weigh(table, slot(PLANE * rr, rr, nb) - cap_f, rows, nb, 128)

        @pl.when(zs == z)
        def _():
            own_f[...] = part_f
            own_b[...] = part_b

        @pl.when(zs != z)
        def _():
            send_p[zs, 0:nf, :] = part_f.astype(BF)
            send_p[zs, nf : nf + nb, :] = part_b.astype(BF)
            part_copy(zs).start()

    def step(k, carry):
        @pl.when(k < depth)
        def _():
            zs = source(k)

            @pl.when((zs != z) & jnp.logical_not(passes_through(zs)))
            def _():
                relay(zs, 0).wait_recv()

            @pl.when(k == 0)
            def _():
                send_on(zs)
                for copy in weight_copies:
                    copy.start()

            select(zs)

        @pl.when(k < depth - 1)
        def _():
            after = source(k + 1)

            @pl.when(passes_through(after))
            def _():
                relay(after, 0).wait_recv()
                send_on(after)

        @pl.when((k >= 2) & (k <= depth + 1))
        def _():
            @pl.when(k == 2)
            def _():
                for load in loads[3:]:
                    load.wait()
                for copy in weight_copies:
                    copy.wait_recv()

            expert(source((k - 1) % depth))

        @pl.when(k >= 3)
        def _():
            combine(source((k - 2) % depth))

        return carry

    lax.fori_loop(0, depth + 3, step, 0)

    total_f = blocks[z, row_f : row_f + nf, :].astype(F32)
    total_b = blocks[z, row_g : row_g + nb, :].astype(F32)
    for q in range(1, depth):
        zs = (z + q) % depth
        part_arrival(zs).wait_recv()
        total_f = total_f + recv_p[zs, 0:nf, :].astype(F32)
        total_b = total_b + recv_p[zs, nf : nf + nb, :].astype(F32)
    out_f[...] = (total_f + own_f[...]).astype(BF)
    out_b[...] = (total_b + own_b[...]).astype(BF)

    for copy in weight_copies:
        copy.wait_send()

    def drain(zs, carry):
        @pl.when(goes_right(zs))
        def _():
            relay(zs, 1).wait_send()

        @pl.when(goes_left(zs))
        def _():
            relay(zs, 0).wait_send()

        for q in range(1, PLANE):
            dispatch_copy(zs, q).wait_send()
            return_copy(zs, q).wait_send()

        @pl.when(zs != z)
        def _():
            part_copy(zs).wait_send()

        return carry

    lax.fori_loop(0, depth, drain, 0)


def place(ahead, back, out_ahead, out_back, sem):
    copies = [
        pltpu.make_async_copy(ahead, out_ahead, sem.at[0]),
        pltpu.make_async_copy(back, out_back, sem.at[1]),
    ]
    for copy in copies:
        copy.start()
    for copy in copies:
        copy.wait()


def passed_along(block, axis, distance):
    count = lax.axis_size(axis)
    if count == 1:
        return block
    route = [((i - distance) % count, i) for i in range(count)]
    return lax.ppermute(block, axis, route)


def on_device(
    forward_input, forward_routes, forward_gates,
    backward_input, backward_routes, backward_gates,
    output_grad, weight_in, weight_down,
):
    devices = lax.axis_size("expert")
    experts = devices // 2
    depth = experts // PLANE
    nf, width = forward_input.shape[1:]
    nb = backward_input.shape[1]
    half = weight_down.shape[2]
    cap_f = 2 * (7 * nf // (2 * experts))
    cap_b = 2 * (7 * nb // (2 * experts))
    rf, rp, rb = up16(cap_f), up16(2 * cap_b), up16(cap_b)
    rr = up16(cap_f + cap_b)
    tables = [
        jnp.transpose(array, (2, 0, 1))
        for array in (forward_routes, forward_gates, backward_routes, backward_gates)
    ]
    vmem = pl.BlockSpec(memory_space=pltpu.VMEM)
    anywhere = pl.BlockSpec(memory_space=pl.ANY)
    hbm = pl.BlockSpec(memory_space=pltpu.HBM)
    dma = pltpu.SemaphoreType.DMA
    ahead, back = pl.pallas_call(
        functools.partial(kernel, depth, experts, cap_f, cap_b),
        out_shape=(
            jax.ShapeDtypeStruct((nf, width), BF),
            jax.ShapeDtypeStruct((nb, width), BF),
        ),
        in_specs=[vmem] * 4 + [anywhere] * 5,
        out_specs=(vmem, vmem),
        scratch_shapes=[
            pltpu.VMEM((depth, experts + 2 * nb + nf, width), BF),
            pltpu.VMEM((depth, PLANE, rf + rp, width), BF),
            pltpu.VMEM((depth, PLANE, rf + rp, width), BF),
            pltpu.VMEM((depth, PLANE, rr, width), BF),
            pltpu.VMEM((depth, PLANE, rr, width), BF),
            pltpu.VMEM((depth, nf + nb, width), BF),
            pltpu.VMEM((depth, nf + nb, width), BF),
            pltpu.VMEM((PLANE * (rf + 2 * rb), width), BF),
            pltpu.VMEM((PLANE * rf, width), F32),
            pltpu.VMEM((PLANE * rb, width), F32),
            pltpu.VMEM((nf, width), F32),
            pltpu.VMEM((nb, width), F32),
            pltpu.VMEM((2, width, 2 * half), BF),
            pltpu.VMEM((2, half, width), BF),
            dma((5,)),
            dma((2,)),
            dma((2,)),
            dma((depth, 2)),
            dma((depth,)),
            dma((depth, PLANE)),
            dma((depth, PLANE)),
            dma((depth, PLANE)),
            dma((depth, PLANE)),
            dma((depth,)),
            dma((depth,)),
        ],
        compiler_params=pltpu.CompilerParams(
            collective_id=0, has_side_effects=True, vmem_limit_bytes=56 * 1024 * 1024
        ),
    )(
        *tables, forward_input[0], backward_input[0], output_grad[0],
        weight_in[0, 0], weight_down[0, 0],
    )
    if lax.axis_size("section") == 1:
        ahead, back = pl.pallas_call(
            place,
            out_shape=(
                jax.ShapeDtypeStruct((nf, width), BF),
                jax.ShapeDtypeStruct((nb, width), BF),
            ),
            in_specs=[hbm] * 2,
            out_specs=(hbm, hbm),
            scratch_shapes=[dma((2,))],
        )(ahead, back)
    forward_sent = passed_along(ahead[None], "section", 1)
    backward_sent = passed_along(back[None], "section", -1)
    return (forward_sent, backward_sent)


def solution(mesh):
    rows = P("section", "expert", None)
    weights = P("section", "expert", None, None)
    return jax.shard_map(
        on_device,
        mesh=mesh,
        in_specs=(rows,) * 7 + (weights,) * 2,
        out_specs=(rows, rows),
        check_vma=False,
    )
```

```python
import functools
import jax
import jax.numpy as jnp
from jax import lax
from jax.experimental import pallas as pl
from jax.experimental.pallas import tpu as pltpu
from jax.sharding import PartitionSpec as P

PLANE = 4
NONE = -512.0
BF = jnp.bfloat16
F32 = jnp.float32
MESH = pl.DeviceIdType.MESH


def up16(count):
    return -(-count // 16) * 16


def dot(a, b):
    return jnp.dot(a, b, preferred_element_type=F32)


def dot_t(a, b):
    return lax.dot_general(a, b, (((1,), (1,)), ((), ())), preferred_element_type=F32)


def t_dot(a, b):
    return lax.dot_general(a, b, (((0,), (0,)), ((), ())), preferred_element_type=F32)


def iota(shape, dim):
    return lax.broadcasted_iota(jnp.int32, shape, dim)


def kernel(
    depth, experts, cap_f, cap_b,
    routes_f, gates_f, routes_b, gates_b, tok_f, tok_b, grad_b, w_in, w_down,
    out_f, out_b,
    blocks, send_d, recv_d, send_t, recv_t, send_r, recv_r, send_p, recv_p,
    mine, acc, own_f, own_b, wi, wd, order, packing,
    sem_load, sem_ws, sem_wr, sem_gs, sem_gr, sem_ds, sem_dr, sem_ts, sem_tr, sem_rs, sem_rr, sem_ps, sem_pr,
):
    nf, width = tok_f.shape
    nb = tok_b.shape[0]
    half = w_down.shape[0]
    whole = (cap_f + 2 * cap_b) // 16 * 16
    rest = cap_f + 2 * cap_b - whole
    folds = width // 128
    rt = folds * rest
    mf, mb = up16(PLANE * cap_f), up16(PLANE * cap_b)
    rr = up16(cap_f + cap_b)
    sec = lax.axis_index("section")
    me = lax.axis_index("expert")
    c = me % 2
    p = (me // 2) % PLANE
    z = me // (2 * PLANE)

    def dev(zz, pp, cc):
        return (sec, (zz * PLANE + pp) * 2 + cc)

    row_b, row_g, row_f = experts, experts + nb, experts + 2 * nb
    loads = [
        pltpu.make_async_copy(tok_b, blocks.at[z, pl.ds(row_b, nb)], sem_load.at[0]),
        pltpu.make_async_copy(grad_b, blocks.at[z, pl.ds(row_g, nb)], sem_load.at[1]),
        pltpu.make_async_copy(tok_f, blocks.at[z, pl.ds(row_f, nf)], sem_load.at[2]),
        pltpu.make_async_copy(w_in, wi.at[c], sem_load.at[3]),
        pltpu.make_async_copy(w_down, wd.at[c], sem_load.at[4]),
    ]
    for load in loads:
        load.start()

    barrier = pltpu.get_barrier_semaphore()
    pl.semaphore_signal(barrier, inc=1, device_id=dev(z, p, 1 - c), device_id_type=MESH)
    for q in range(1, PLANE):
        pl.semaphore_signal(
            barrier, inc=1, device_id=dev(z, (p + q) % PLANE, c), device_id_type=MESH
        )
    for q in range(1, depth):
        pl.semaphore_signal(
            barrier, inc=1, device_id=dev((z + q) % depth, p, c), device_id_type=MESH
        )

    for load in loads[:3]:
        load.wait()
    lanes = 256
    blocks[z, 0:experts, :] = jnp.zeros((experts, width), BF)
    for routes, gates, lane in ((routes_f, gates_f, 0), (routes_b, gates_b, 128)):
        count = routes.shape[2]
        e_ids = iota((experts, count), 0)
        named = jnp.zeros((experts, count), F32)
        weight = jnp.zeros((experts, count), F32)
        for k in range(routes.shape[0]):
            hit = routes[k] == e_ids
            named = named + jnp.where(hit, 1.0, 0.0)
            weight = weight + jnp.where(hit, gates[k], 0.0)
        earlier = jnp.where(iota((count, count), 0) < iota((count, count), 1), 1.0, 0.0)
        rank = dot(named.astype(BF), earlier.astype(BF))
        high = weight.astype(BF)
        low = (weight - high.astype(F32)).astype(BF)
        code = jnp.where(named > 0.0, rank, NONE).astype(BF)
        for part, values in enumerate((code, high, low)):
            start = part * lanes + lane
            blocks[z, 0:experts, start : start + count] = values

    weight_copies = [
        pltpu.make_async_remote_copy(
            w_in, wi.at[c], sem_ws.at[0], sem_wr.at[0], device_id=dev(z, p, 1 - c), device_id_type=MESH
        ),
        pltpu.make_async_remote_copy(
            w_down, wd.at[c], sem_ws.at[1], sem_wr.at[1], device_id=dev(z, p, 1 - c), device_id_type=MESH
        ),
    ]
    def source(k):
        near = jnp.minimum(z, depth - 1 - z)
        side = jnp.where(k % 2 == 1, z - (k + 1) // 2, z + k // 2)
        far = jnp.where(2 * z < depth, k, depth - 1 - k)
        return jnp.where(k <= 2 * near, side, far)

    def relay(zs, way):
        return pltpu.make_async_remote_copy(
            blocks.at[zs], blocks.at[zs], sem_gs.at[zs, way], sem_gr.at[zs],
            device_id=dev((z + 1 if way else z + depth - 1) % depth, p, c), device_id_type=MESH,
        )

    def goes_right(zs):
        return (zs <= z) & (z < depth - 1)

    def goes_left(zs):
        return (zs >= z) & (z > 0)

    def passes_through(zs):
        return (zs != z) & (goes_right(zs) | goes_left(zs))

    def send_on(zs):
        @pl.when(goes_right(zs))
        def _():
            relay(zs, 1).start()

        @pl.when(goes_left(zs))
        def _():
            relay(zs, 0).start()

    def dispatch_copy(zs, q):
        tgt = (p + q) % PLANE
        return pltpu.make_async_remote_copy(
            send_d.at[zs, tgt], recv_d.at[zs, p], sem_ds.at[zs, q], sem_dr.at[zs, p],
            device_id=dev(z, tgt, c), device_id_type=MESH,
        )

    def dispatch_arrival(zs, q):
        other = (p + q) % PLANE
        return pltpu.make_async_remote_copy(
            send_d.at[zs, other], recv_d.at[zs, other], sem_ds.at[zs, q], sem_dr.at[zs, other],
            device_id=dev(z, other, c), device_id_type=MESH,
        )

    def return_copy(zs, q):
        tgt = (p + q) % PLANE
        return pltpu.make_async_remote_copy(
            send_r.at[zs, tgt], recv_r.at[zs, p], sem_rs.at[zs, q], sem_rr.at[zs, p],
            device_id=dev(z, tgt, c), device_id_type=MESH,
        )

    def return_arrival(zs, q):
        other = (p + q) % PLANE
        return pltpu.make_async_remote_copy(
            send_r.at[zs, other], recv_r.at[zs, other], sem_rs.at[zs, q], sem_rr.at[zs, other],
            device_id=dev(z, other, c), device_id_type=MESH,
        )

    def part_copy(zs):
        return pltpu.make_async_remote_copy(
            send_p.at[zs], recv_p.at[z], sem_ps.at[zs], sem_pr.at[z],
            device_id=dev(zs, p, c), device_id_type=MESH,
        )

    def part_arrival(zs):
        return pltpu.make_async_remote_copy(
            send_p.at[zs], recv_p.at[zs], sem_ps.at[zs], sem_pr.at[zs],
            device_id=dev(zs, p, c), device_id_type=MESH,
        )

    def spread(zs, rows):
        total = PLANE * rows
        pick = jnp.where(
            iota((total, experts), 1) == z * PLANE + iota((total, experts), 0) // rows, 1.0, 0.0
        ).astype(BF)
        return dot(pick, blocks[zs, 0:experts, 0 : 3 * lanes])

    def slot(total, rows, count):
        return (iota((total, count), 0) % rows).astype(F32)

    def tail_copy(zs, q):
        tgt = (p + q) % PLANE
        return pltpu.make_async_remote_copy(
            send_t.at[zs, tgt], recv_t.at[zs, p], sem_ts.at[zs, q], sem_tr.at[zs, p],
            device_id=dev(z, tgt, c), device_id_type=MESH,
        )

    def tail_arrival(zs, q):
        other = (p + q) % PLANE
        return pltpu.make_async_remote_copy(
            send_t.at[zs, other], recv_t.at[zs, other], sem_ts.at[zs, q], sem_tr.at[zs, other],
            device_id=dev(z, other, c), device_id_type=MESH,
        )

    def one_hot(hit):
        return jnp.where(hit, 1.0, 0.0).astype(BF)

    def select(zs):
        table = spread(zs, whole)
        table_f, table_b = table[:, 0:nf], table[:, 128 : 128 + nb]
        place_f, place_b = slot(PLANE * whole, whole, nf), slot(PLANE * whole, whole, nb)
        x = blocks[zs, row_b : row_b + nb, :]
        g = blocks[zs, row_g : row_g + nb, :]
        rows = (
            dot(one_hot(table_f == place_f), blocks[zs, row_f : row_f + nf, :])
            + dot(one_hot(table_b + cap_f == place_b), x)
            + dot(one_hot(table_b + (cap_f + cap_b) == place_b), g)
        ).astype(BF)
        table_t = spread(zs, rt)[:, 128 : 128 + nb]
        place_t = (iota((PLANE * rt, nb), 0) % rest + whole).astype(F32)
        wide = dot(one_hot(table_t + (cap_f + cap_b) == place_t), g)
        fold = iota((PLANE * rt, 128), 0) % rt // rest
        tail = jnp.zeros((PLANE * rt, 128), F32)
        for q in range(folds):
            tail = tail + jnp.where(fold == q, wide[:, q * 128 : (q + 1) * 128], 0.0)
        tail = tail.astype(BF)
        for q in range(PLANE):
            send_d[zs, q] = rows[q * whole : (q + 1) * whole]
            send_t[zs, q] = tail[q * rt : (q + 1) * rt]

    def dispatch(zs):
        for q in range(1, PLANE):
            dispatch_copy(zs, q).start()
            tail_copy(zs, q).start()
        recv_d[zs, p] = send_d[zs, p]
        recv_t[zs, p] = send_t[zs, p]

    def arrange():
        for start, size, count, first in (
            (0, mf, cap_f, 0), (mf, mb, cap_b, cap_f), (mf + mb, mb, cap_b, cap_f + cap_b)
        ):
            row, col = iota((size, PLANE * whole), 0), iota((size, PLANE * whole), 1)
            hit = (row // count == col // whole) & (row % count + first == col % whole)
            order[start : start + size] = one_hot(hit)
        for start, size, count, first in ((0, mf, cap_f, 0), (mf, mb, cap_b, cap_f)):
            shape = (PLANE * rr, size)
            row, col = iota(shape, 0), iota(shape, 1)
            hit = (row // rr == col // count) & (row % rr == col % count + first)
            packing[:, start : start + size] = one_hot(hit)

    def expert(zs, is_first):
        for q in range(1, PLANE):
            dispatch_arrival(zs, q).wait_recv()
            tail_arrival(zs, q).wait_recv()
        rows = dot(order[...], recv_d[zs].reshape(PLANE * whole, width))
        tail = recv_t[zs].reshape(PLANE * rt, 128)
        fold = iota((PLANE * rt, 128), 0) % rt // rest
        wide = jnp.concatenate(
            [jnp.where(fold == q, tail, jnp.zeros_like(tail)) for q in range(folds)], axis=1
        )
        row, col = iota((mb, PLANE * rt), 0), iota((mb, PLANE * rt), 1)
        hit = (row // cap_b == col // rt) & (
            row % cap_b + (cap_f + cap_b) == col % rest + whole
        )
        mine[0 : mf + mb] = rows[0 : mf + mb].astype(BF)
        mine[mf + mb :] = (rows[mf + mb :] + dot(one_hot(hit), wide)).astype(BF)

        def one_half(i, carry):
            h = (c + i) % 2

            @pl.when(is_first & (i == 0))
            def _():
                for load in loads[3:]:
                    load.wait()

            @pl.when(is_first & (i == 1))
            def _():
                for copy in weight_copies:
                    copy.wait_recv()

            hidden = dot(mine[0 : mf + mb], wi[h])
            a, b = hidden[:, :half], hidden[:, half:]
            q = jax.nn.sigmoid(a)
            active = (a[:mf] * q[:mf] * b[:mf]).astype(BF)
            part_f = dot(active, wd[h])
            u = dot_t(mine[mf + mb : mf + 2 * mb], wd[h])
            a, b, q = a[mf:], b[mf:], q[mf:]
            grad = jnp.concatenate([u * b * q * (1.0 + a * (1.0 - q)), u * a * q], axis=1)
            part_b = dot_t(grad.astype(BF), wi[h])

            @pl.when(i == 0)
            def _():
                acc[0:mf] = part_f
                acc[mf : mf + mb] = part_b

            @pl.when(i == 1)
            def _():
                acc[0:mf] = acc[0:mf] + part_f
                acc[mf : mf + mb] = acc[mf : mf + mb] + part_b

            return carry

        lax.fori_loop(0, 2, one_half, 0)
        packed = dot(packing[...], acc[...].astype(BF)).astype(BF)
        for j in range(PLANE):
            send_r[zs, j] = packed[j * rr : (j + 1) * rr]
        for q in range(1, PLANE):
            return_copy(zs, q).start()
        recv_r[zs, p] = send_r[zs, p]

    def weigh(table, place, rows, count, lane):
        hit = table[:, lane : lane + count] == place
        high_part = jnp.where(hit, table[:, lanes + lane : lanes + lane + count], 0.0)
        low_part = jnp.where(hit, table[:, 2 * lanes + lane : 2 * lanes + lane + count], 0.0)
        return t_dot(high_part.astype(BF), rows) + t_dot(low_part.astype(BF), rows)

    def combine(zs):
        for q in range(1, PLANE):
            return_arrival(zs, q).wait_recv()
        rows = recv_r[zs].reshape(PLANE * rr, width)
        table = spread(zs, rr)
        part_f = weigh(table, slot(PLANE * rr, rr, nf), rows, nf, 0)
        part_b = weigh(table, slot(PLANE * rr, rr, nb) - cap_f, rows, nb, 128)

        @pl.when(zs == z)
        def _():
            own_f[...] = part_f
            own_b[...] = part_b

        @pl.when(zs != z)
        def _():
            send_p[zs, 0:nf, :] = part_f.astype(BF)
            send_p[zs, nf : nf + nb, :] = part_b.astype(BF)
            part_copy(zs).start()

    def pass_on(zs):
        @pl.when(passes_through(zs))
        def _():
            relay(zs, 0).wait_recv()
            send_on(zs)

    def step(k, carry):
        @pl.when(k < depth)
        def _():
            zs = source(k)

            @pl.when(jnp.logical_not(passes_through(zs)))
            def _():
                relay(zs, 0).wait_recv()

            select(zs)
            dispatch(zs)

        @pl.when(k < depth - 1)
        def _():
            pass_on(source(k + 1))

        @pl.when((k >= 2) & (k <= depth + 1))
        def _():
            expert(source((k - 1) % depth), k == 2)

        @pl.when(k >= 3)
        def _():
            combine(source((k - 2) % depth))

        return carry

    select(z)
    pl.semaphore_wait(barrier, 1 + (PLANE - 1) + (depth - 1))
    send_on(z)
    dispatch(z)
    for copy in weight_copies:
        copy.start()
    arrange()
    pass_on(source(1))
    lax.fori_loop(1, depth + 3, step, 0)

    total_f = blocks[z, row_f : row_f + nf, :].astype(F32)
    total_b = blocks[z, row_g : row_g + nb, :].astype(F32)
    for q in range(1, depth):
        zs = (z + q) % depth
        part_arrival(zs).wait_recv()
        total_f = total_f + recv_p[zs, 0:nf, :].astype(F32)
        total_b = total_b + recv_p[zs, nf : nf + nb, :].astype(F32)
    out_f[...] = (total_f + own_f[...]).astype(BF)
    out_b[...] = (total_b + own_b[...]).astype(BF)

    for copy in weight_copies:
        copy.wait_send()

    def drain(zs, carry):
        @pl.when(goes_right(zs))
        def _():
            relay(zs, 1).wait_send()

        @pl.when(goes_left(zs))
        def _():
            relay(zs, 0).wait_send()

        for q in range(1, PLANE):
            dispatch_copy(zs, q).wait_send()
            tail_copy(zs, q).wait_send()
            return_copy(zs, q).wait_send()

        @pl.when(zs != z)
        def _():
            part_copy(zs).wait_send()

        return carry

    lax.fori_loop(0, depth, drain, 0)


def passed_along(block, axis, distance):
    count = lax.axis_size(axis)
    if count == 1:
        return block
    route = [((i - distance) % count, i) for i in range(count)]
    return lax.ppermute(block, axis, route)


def on_device(
    forward_input, forward_routes, forward_gates,
    backward_input, backward_routes, backward_gates,
    output_grad, weight_in, weight_down,
):
    devices = lax.axis_size("expert")
    experts = devices // 2
    depth = experts // PLANE
    nf, width = forward_input.shape[1:]
    nb = backward_input.shape[1]
    half = weight_down.shape[2]
    cap_f = 2 * (7 * nf // (2 * experts))
    cap_b = 2 * (7 * nb // (2 * experts))
    whole = (cap_f + 2 * cap_b) // 16 * 16
    rt = (cap_f + 2 * cap_b - whole) * (width // 128)
    mf, mb = up16(PLANE * cap_f), up16(PLANE * cap_b)
    rr = up16(cap_f + cap_b)
    tables = [
        jnp.transpose(array, (2, 0, 1))
        for array in (forward_routes, forward_gates, backward_routes, backward_gates)
    ]
    vmem = pl.BlockSpec(memory_space=pltpu.VMEM)
    anywhere = pl.BlockSpec(memory_space=pl.ANY)
    dma = pltpu.SemaphoreType.DMA
    ahead, back = pl.pallas_call(
        functools.partial(kernel, depth, experts, cap_f, cap_b),
        out_shape=(
            jax.ShapeDtypeStruct((nf, width), BF),
            jax.ShapeDtypeStruct((nb, width), BF),
        ),
        in_specs=[vmem] * 4 + [anywhere] * 5,
        out_specs=(vmem, vmem),
        scratch_shapes=[
            pltpu.VMEM((depth, experts + 2 * nb + nf, width), BF),
            pltpu.VMEM((depth, PLANE, whole, width), BF),
            pltpu.VMEM((depth, PLANE, whole, width), BF),
            pltpu.VMEM((depth, PLANE, rt, 128), BF),
            pltpu.VMEM((depth, PLANE, rt, 128), BF),
            pltpu.VMEM((depth, PLANE, rr, width), BF),
            pltpu.VMEM((depth, PLANE, rr, width), BF),
            pltpu.VMEM((depth, nf + nb, width), BF),
            pltpu.VMEM((depth, nf + nb, width), BF),
            pltpu.VMEM((mf + 2 * mb, width), BF),
            pltpu.VMEM((mf + mb, width), F32),
            pltpu.VMEM((nf, width), F32),
            pltpu.VMEM((nb, width), F32),
            pltpu.VMEM((2, width, 2 * half), BF),
            pltpu.VMEM((2, half, width), BF),
            pltpu.VMEM((mf + 2 * mb, PLANE * whole), BF),
            pltpu.VMEM((PLANE * rr, mf + mb), BF),
            dma((5,)),
            dma((2,)),
            dma((2,)),
            dma((depth, 2)),
            dma((depth,)),
            dma((depth, PLANE)),
            dma((depth, PLANE)),
            dma((depth, PLANE)),
            dma((depth, PLANE)),
            dma((depth, PLANE)),
            dma((depth, PLANE)),
            dma((depth,)),
            dma((depth,)),
        ],
        compiler_params=pltpu.CompilerParams(
            collective_id=0, has_side_effects=True, vmem_limit_bytes=56 * 1024 * 1024
        ),
    )(
        *tables, forward_input[0], backward_input[0], output_grad[0],
        weight_in[0, 0], weight_down[0, 0],
    )
    forward_sent = passed_along(ahead[None], "section", 1)
    backward_sent = passed_along(back[None], "section", -1)
    return (forward_sent, backward_sent)


def solution(mesh):
    rows = P("section", "expert", None)
    weights = P("section", "expert", None, None)
    return jax.shard_map(
        on_device,
        mesh=mesh,
        in_specs=(rows,) * 7 + (weights,) * 2,
        out_specs=(rows, rows),
        check_vma=False,
    )
```

```python
import functools
import jax
import jax.numpy as jnp
from jax import lax
from jax.experimental import pallas as pl
from jax.experimental.pallas import tpu as pltpu
from jax.sharding import PartitionSpec as P

PLANE = 4
NONE = -512.0
BF = jnp.bfloat16
F32 = jnp.float32
MESH = pl.DeviceIdType.MESH


def up16(count):
    return -(-count // 16) * 16


def dot(a, b):
    return jnp.dot(a, b, preferred_element_type=F32)


def dot_t(a, b):
    return lax.dot_general(a, b, (((1,), (1,)), ((), ())), preferred_element_type=F32)


def t_dot(a, b):
    return lax.dot_general(a, b, (((0,), (0,)), ((), ())), preferred_element_type=F32)


def iota(shape, dim):
    return lax.broadcasted_iota(jnp.int32, shape, dim)


def kernel(
    depth, experts, cap_f, cap_b,
    routes_f, gates_f, routes_b, gates_b, tok_f, tok_b, grad_b, w_in, w_down,
    out_f, out_b,
    blocks, send_d, recv_d, send_t, recv_t, send_r, recv_r, send_p, recv_p,
    mine, acc, own_f, own_b, wi, wd, order, packing,
    sem_load, sem_ws, sem_wr, sem_gs, sem_gr, sem_ds, sem_dr, sem_ts, sem_tr, sem_rs, sem_rr, sem_ps, sem_pr,
):
    nf, width = tok_f.shape
    nb = tok_b.shape[0]
    half = w_down.shape[0]
    whole = (cap_f + 2 * cap_b) // 16 * 16
    rest = cap_f + 2 * cap_b - whole
    folds = width // 128
    rt = folds * rest
    mf, mb = up16(PLANE * cap_f), up16(PLANE * cap_b)
    rr = up16(cap_f + cap_b)
    sec = lax.axis_index("section")
    me = lax.axis_index("expert")
    c = me % 2
    p = (me // 2) % PLANE
    z = me // (2 * PLANE)

    def dev(zz, pp, cc):
        return (sec, (zz * PLANE + pp) * 2 + cc)

    row_b, row_g, row_f = experts, experts + nb, experts + 2 * nb
    loads = [
        pltpu.make_async_copy(tok_b, blocks.at[z, pl.ds(row_b, nb)], sem_load.at[0]),
        pltpu.make_async_copy(grad_b, blocks.at[z, pl.ds(row_g, nb)], sem_load.at[1]),
        pltpu.make_async_copy(tok_f, blocks.at[z, pl.ds(row_f, nf)], sem_load.at[2]),
        pltpu.make_async_copy(w_in, wi.at[c], sem_load.at[3]),
        pltpu.make_async_copy(w_down, wd.at[c], sem_load.at[4]),
    ]
    for load in loads:
        load.start()

    barrier = pltpu.get_barrier_semaphore()
    pl.semaphore_signal(barrier, inc=1, device_id=dev(z, p, 1 - c), device_id_type=MESH)
    for q in range(1, PLANE):
        pl.semaphore_signal(
            barrier, inc=1, device_id=dev(z, (p + q) % PLANE, c), device_id_type=MESH
        )
    for q in range(1, depth):
        pl.semaphore_signal(
            barrier, inc=1, device_id=dev((z + q) % depth, p, c), device_id_type=MESH
        )

    for load in loads[:3]:
        load.wait()
    lanes = 256
    blocks[z, 0:experts, :] = jnp.zeros((experts, width), BF)
    for routes, gates, lane in ((routes_f, gates_f, 0), (routes_b, gates_b, 128)):
        count = routes.shape[2]
        e_ids = iota((experts, count), 0)
        named = jnp.zeros((experts, count), F32)
        weight = jnp.zeros((experts, count), F32)
        for k in range(routes.shape[0]):
            hit = routes[k] == e_ids
            named = named + jnp.where(hit, 1.0, 0.0)
            weight = weight + jnp.where(hit, gates[k], 0.0)
        earlier = jnp.where(iota((count, count), 0) < iota((count, count), 1), 1.0, 0.0)
        rank = dot(named.astype(BF), earlier.astype(BF))
        high = weight.astype(BF)
        low = (weight - high.astype(F32)).astype(BF)
        code = jnp.where(named > 0.0, rank, NONE).astype(BF)
        for part, values in enumerate((code, high, low)):
            start = part * lanes + lane
            blocks[z, 0:experts, start : start + count] = values

    weight_copies = [
        pltpu.make_async_remote_copy(
            w_in, wi.at[c], sem_ws.at[0], sem_wr.at[0], device_id=dev(z, p, 1 - c), device_id_type=MESH
        ),
        pltpu.make_async_remote_copy(
            w_down, wd.at[c], sem_ws.at[1], sem_wr.at[1], device_id=dev(z, p, 1 - c), device_id_type=MESH
        ),
    ]
    def source(k):
        near = jnp.minimum(z, depth - 1 - z)
        side = jnp.where(k % 2 == 1, z - (k + 1) // 2, z + k // 2)
        far = jnp.where(2 * z < depth, k, depth - 1 - k)
        return jnp.where(k <= 2 * near, side, far)

    def relay(zs, way):
        return pltpu.make_async_remote_copy(
            blocks.at[zs], blocks.at[zs], sem_gs.at[zs, way], sem_gr.at[zs],
            device_id=dev((z + 1 if way else z + depth - 1) % depth, p, c), device_id_type=MESH,
        )

    def goes_right(zs):
        return (zs <= z) & (z < depth - 1)

    def goes_left(zs):
        return (zs >= z) & (z > 0)

    def passes_through(zs):
        return (zs != z) & (goes_right(zs) | goes_left(zs))

    def send_on(zs):
        @pl.when(goes_right(zs))
        def _():
            relay(zs, 1).start()

        @pl.when(goes_left(zs))
        def _():
            relay(zs, 0).start()

    def dispatch_copy(zs, q):
        tgt = (p + q) % PLANE
        return pltpu.make_async_remote_copy(
            send_d.at[zs, tgt], recv_d.at[zs, p], sem_ds.at[zs, q], sem_dr.at[zs, p],
            device_id=dev(z, tgt, c), device_id_type=MESH,
        )

    def dispatch_arrival(zs, q):
        other = (p + q) % PLANE
        return pltpu.make_async_remote_copy(
            send_d.at[zs, other], recv_d.at[zs, other], sem_ds.at[zs, q], sem_dr.at[zs, other],
            device_id=dev(z, other, c), device_id_type=MESH,
        )

    def return_copy(zs, q):
        tgt = (p + q) % PLANE
        return pltpu.make_async_remote_copy(
            send_r.at[zs, tgt], recv_r.at[zs, p], sem_rs.at[zs, q], sem_rr.at[zs, p],
            device_id=dev(z, tgt, c), device_id_type=MESH,
        )

    def return_arrival(zs, q):
        other = (p + q) % PLANE
        return pltpu.make_async_remote_copy(
            send_r.at[zs, other], recv_r.at[zs, other], sem_rs.at[zs, q], sem_rr.at[zs, other],
            device_id=dev(z, other, c), device_id_type=MESH,
        )

    def part_copy(zs):
        return pltpu.make_async_remote_copy(
            send_p.at[zs], recv_p.at[z], sem_ps.at[zs], sem_pr.at[z],
            device_id=dev(zs, p, c), device_id_type=MESH,
        )

    def part_arrival(zs):
        return pltpu.make_async_remote_copy(
            send_p.at[zs], recv_p.at[zs], sem_ps.at[zs], sem_pr.at[zs],
            device_id=dev(zs, p, c), device_id_type=MESH,
        )

    def spread(zs, rows):
        total = PLANE * rows
        pick = jnp.where(
            iota((total, experts), 1) == z * PLANE + iota((total, experts), 0) // rows, 1.0, 0.0
        ).astype(BF)
        return dot(pick, blocks[zs, 0:experts, 0 : 3 * lanes])

    def slot(total, rows, count):
        return (iota((total, count), 0) % rows).astype(F32)

    def tail_copy(zs, q):
        tgt = (p + q) % PLANE
        return pltpu.make_async_remote_copy(
            send_t.at[zs, tgt], recv_t.at[zs, p], sem_ts.at[zs, q], sem_tr.at[zs, p],
            device_id=dev(z, tgt, c), device_id_type=MESH,
        )

    def tail_arrival(zs, q):
        other = (p + q) % PLANE
        return pltpu.make_async_remote_copy(
            send_t.at[zs, other], recv_t.at[zs, other], sem_ts.at[zs, q], sem_tr.at[zs, other],
            device_id=dev(z, other, c), device_id_type=MESH,
        )

    def one_hot(hit):
        return jnp.where(hit, 1.0, 0.0).astype(BF)

    def select(zs):
        table = spread(zs, whole)
        table_f, table_b = table[:, 0:nf], table[:, 128 : 128 + nb]
        place_f, place_b = slot(PLANE * whole, whole, nf), slot(PLANE * whole, whole, nb)
        x = blocks[zs, row_b : row_b + nb, :]
        g = blocks[zs, row_g : row_g + nb, :]
        rows = (
            dot(one_hot(table_f == place_f), blocks[zs, row_f : row_f + nf, :])
            + dot(one_hot(table_b + cap_f == place_b), x)
            + dot(one_hot(table_b + (cap_f + cap_b) == place_b), g)
        ).astype(BF)
        table_t = spread(zs, rt)[:, 128 : 128 + nb]
        place_t = (iota((PLANE * rt, nb), 0) % rest + whole).astype(F32)
        wide = dot(one_hot(table_t + (cap_f + cap_b) == place_t), g)
        fold = iota((PLANE * rt, 128), 0) % rt // rest
        tail = jnp.zeros((PLANE * rt, 128), F32)
        for q in range(folds):
            tail = tail + jnp.where(fold == q, wide[:, q * 128 : (q + 1) * 128], 0.0)
        tail = tail.astype(BF)
        for q in range(PLANE):
            send_d[zs, q] = rows[q * whole : (q + 1) * whole]
            send_t[zs, q] = tail[q * rt : (q + 1) * rt]

    def dispatch(zs):
        for q in range(1, PLANE):
            dispatch_copy(zs, q).start()
            tail_copy(zs, q).start()
        recv_d[zs, p] = send_d[zs, p]
        recv_t[zs, p] = send_t[zs, p]

    def arrange():
        for start, size, count, first in (
            (0, mf, cap_f, 0), (mf, mb, cap_b, cap_f), (mf + mb, mb, cap_b, cap_f + cap_b)
        ):
            row, col = iota((size, PLANE * whole), 0), iota((size, PLANE * whole), 1)
            hit = (row // count == col // whole) & (row % count + first == col % whole)
            order[start : start + size] = one_hot(hit)
        for start, size, count, first in ((0, mf, cap_f, 0), (mf, mb, cap_b, cap_f)):
            shape = (PLANE * rr, size)
            row, col = iota(shape, 0), iota(shape, 1)
            hit = (row // rr == col // count) & (row % rr == col % count + first)
            packing[:, start : start + size] = one_hot(hit)

    def expert(zs, is_first):
        for q in range(1, PLANE):
            dispatch_arrival(zs, q).wait_recv()
            tail_arrival(zs, q).wait_recv()
        rows = dot(order[...], recv_d[zs].reshape(PLANE * whole, width))
        tail = recv_t[zs].reshape(PLANE * rt, 128)
        fold = iota((PLANE * rt, 128), 0) % rt // rest
        wide = jnp.concatenate(
            [jnp.where(fold == q, tail, jnp.zeros_like(tail)) for q in range(folds)], axis=1
        )
        row, col = iota((mb, PLANE * rt), 0), iota((mb, PLANE * rt), 1)
        hit = (row // cap_b == col // rt) & (
            row % cap_b + (cap_f + cap_b) == col % rest + whole
        )
        mine[0 : mf + mb] = rows[0 : mf + mb].astype(BF)
        mine[mf + mb :] = (rows[mf + mb :] + dot(one_hot(hit), wide)).astype(BF)

        def one_half(i, carry):
            h = (c + i) % 2

            @pl.when(is_first & (i == 0))
            def _():
                for load in loads[3:]:
                    load.wait()

            @pl.when(is_first & (i == 1))
            def _():
                for copy in weight_copies:
                    copy.wait_recv()

            hidden = dot(mine[0 : mf + mb], wi[h])
            a, b = hidden[:, :half], hidden[:, half:]
            q = jax.nn.sigmoid(a)
            active = (a[:mf] * q[:mf] * b[:mf]).astype(BF)
            part_f = dot(active, wd[h])
            u = dot_t(mine[mf + mb : mf + 2 * mb], wd[h])
            a, b, q = a[mf:], b[mf:], q[mf:]
            grad = jnp.concatenate([u * b * q * (1.0 + a * (1.0 - q)), u * a * q], axis=1)
            part_b = dot_t(grad.astype(BF), wi[h])

            @pl.when(i == 0)
            def _():
                acc[0:mf] = part_f
                acc[mf : mf + mb] = part_b

            @pl.when(i == 1)
            def _():
                acc[0:mf] = acc[0:mf] + part_f
                acc[mf : mf + mb] = acc[mf : mf + mb] + part_b

            return carry

        lax.fori_loop(0, 2, one_half, 0)
        packed = dot(packing[...], acc[...].astype(BF)).astype(BF)
        for j in range(PLANE):
            send_r[zs, j] = packed[j * rr : (j + 1) * rr]
        for q in range(1, PLANE):
            return_copy(zs, q).start()
        recv_r[zs, p] = send_r[zs, p]

    def weigh(table, place, rows, count, lane):
        hit = table[:, lane : lane + count] == place
        high_part = jnp.where(hit, table[:, lanes + lane : lanes + lane + count], 0.0)
        low_part = jnp.where(hit, table[:, 2 * lanes + lane : 2 * lanes + lane + count], 0.0)
        return t_dot(high_part.astype(BF), rows) + t_dot(low_part.astype(BF), rows)

    def combine(zs):
        for q in range(1, PLANE):
            return_arrival(zs, q).wait_recv()
        rows = recv_r[zs].reshape(PLANE * rr, width)
        table = spread(zs, rr)
        part_f = weigh(table, slot(PLANE * rr, rr, nf), rows, nf, 0)
        part_b = weigh(table, slot(PLANE * rr, rr, nb) - cap_f, rows, nb, 128)

        @pl.when(zs == z)
        def _():
            own_f[...] = part_f
            own_b[...] = part_b

        @pl.when(zs != z)
        def _():
            send_p[zs, 0:nf, :] = part_f.astype(BF)
            send_p[zs, nf : nf + nb, :] = part_b.astype(BF)
            part_copy(zs).start()

    def pass_on(zs):
        @pl.when(passes_through(zs))
        def _():
            relay(zs, 0).wait_recv()
            send_on(zs)

    def step(k, carry):
        @pl.when(k < depth)
        def _():
            zs = source(k)

            @pl.when(jnp.logical_not(passes_through(zs)))
            def _():
                relay(zs, 0).wait_recv()

            select(zs)
            dispatch(zs)

        @pl.when(k < depth - 1)
        def _():
            pass_on(source(k + 1))

        @pl.when(k >= 3)
        def _():
            combine(source(k - 3))

        @pl.when(k <= depth)
        def _():
            expert(source(k - 1), k == 1)

        return carry

    select(z)
    pl.semaphore_wait(barrier, 1 + (PLANE - 1) + (depth - 1))
    send_on(z)
    dispatch(z)
    for copy in weight_copies:
        copy.start()
    arrange()
    pass_on(source(1))
    lax.fori_loop(1, depth + 3, step, 0)

    total_f = blocks[z, row_f : row_f + nf, :].astype(F32)
    total_b = blocks[z, row_g : row_g + nb, :].astype(F32)
    for q in range(1, depth):
        zs = (z + q) % depth
        part_arrival(zs).wait_recv()
        total_f = total_f + recv_p[zs, 0:nf, :].astype(F32)
        total_b = total_b + recv_p[zs, nf : nf + nb, :].astype(F32)
    out_f[...] = (total_f + own_f[...]).astype(BF)
    out_b[...] = (total_b + own_b[...]).astype(BF)

    for copy in weight_copies:
        copy.wait_send()

    def drain(zs, carry):
        @pl.when(goes_right(zs))
        def _():
            relay(zs, 1).wait_send()

        @pl.when(goes_left(zs))
        def _():
            relay(zs, 0).wait_send()

        for q in range(1, PLANE):
            dispatch_copy(zs, q).wait_send()
            tail_copy(zs, q).wait_send()
            return_copy(zs, q).wait_send()

        @pl.when(zs != z)
        def _():
            part_copy(zs).wait_send()

        return carry

    lax.fori_loop(0, depth, drain, 0)


def passed_along(block, axis, distance):
    count = lax.axis_size(axis)
    if count == 1:
        return block
    route = [((i - distance) % count, i) for i in range(count)]
    return lax.ppermute(block, axis, route)


def on_device(
    forward_input, forward_routes, forward_gates,
    backward_input, backward_routes, backward_gates,
    output_grad, weight_in, weight_down,
):
    devices = lax.axis_size("expert")
    experts = devices // 2
    depth = experts // PLANE
    nf, width = forward_input.shape[1:]
    nb = backward_input.shape[1]
    half = weight_down.shape[2]
    cap_f = 2 * (7 * nf // (2 * experts))
    cap_b = 2 * (7 * nb // (2 * experts))
    whole = (cap_f + 2 * cap_b) // 16 * 16
    rt = (cap_f + 2 * cap_b - whole) * (width // 128)
    mf, mb = up16(PLANE * cap_f), up16(PLANE * cap_b)
    rr = up16(cap_f + cap_b)
    tables = [
        jnp.transpose(array, (2, 0, 1))
        for array in (forward_routes, forward_gates, backward_routes, backward_gates)
    ]
    vmem = pl.BlockSpec(memory_space=pltpu.VMEM)
    anywhere = pl.BlockSpec(memory_space=pl.ANY)
    dma = pltpu.SemaphoreType.DMA
    ahead, back = pl.pallas_call(
        functools.partial(kernel, depth, experts, cap_f, cap_b),
        out_shape=(
            jax.ShapeDtypeStruct((nf, width), BF),
            jax.ShapeDtypeStruct((nb, width), BF),
        ),
        in_specs=[vmem] * 4 + [anywhere] * 5,
        out_specs=(vmem, vmem),
        scratch_shapes=[
            pltpu.VMEM((depth, experts + 2 * nb + nf, width), BF),
            pltpu.VMEM((depth, PLANE, whole, width), BF),
            pltpu.VMEM((depth, PLANE, whole, width), BF),
            pltpu.VMEM((depth, PLANE, rt, 128), BF),
            pltpu.VMEM((depth, PLANE, rt, 128), BF),
            pltpu.VMEM((depth, PLANE, rr, width), BF),
            pltpu.VMEM((depth, PLANE, rr, width), BF),
            pltpu.VMEM((depth, nf + nb, width), BF),
            pltpu.VMEM((depth, nf + nb, width), BF),
            pltpu.VMEM((mf + 2 * mb, width), BF),
            pltpu.VMEM((mf + mb, width), F32),
            pltpu.VMEM((nf, width), F32),
            pltpu.VMEM((nb, width), F32),
            pltpu.VMEM((2, width, 2 * half), BF),
            pltpu.VMEM((2, half, width), BF),
            pltpu.VMEM((mf + 2 * mb, PLANE * whole), BF),
            pltpu.VMEM((PLANE * rr, mf + mb), BF),
            dma((5,)),
            dma((2,)),
            dma((2,)),
            dma((depth, 2)),
            dma((depth,)),
            dma((depth, PLANE)),
            dma((depth, PLANE)),
            dma((depth, PLANE)),
            dma((depth, PLANE)),
            dma((depth, PLANE)),
            dma((depth, PLANE)),
            dma((depth,)),
            dma((depth,)),
        ],
        compiler_params=pltpu.CompilerParams(
            collective_id=0, has_side_effects=True, vmem_limit_bytes=56 * 1024 * 1024
        ),
    )(
        *tables, forward_input[0], backward_input[0], output_grad[0],
        weight_in[0, 0], weight_down[0, 0],
    )
    forward_sent = passed_along(ahead[None], "section", 1)
    backward_sent = passed_along(back[None], "section", -1)
    return (forward_sent, backward_sent)


def solution(mesh):
    rows = P("section", "expert", None)
    weights = P("section", "expert", None, None)
    return jax.shard_map(
        on_device,
        mesh=mesh,
        in_specs=(rows,) * 7 + (weights,) * 2,
        out_specs=(rows, rows),
        check_vma=False,
    )
```

```python
import functools
import jax
import jax.numpy as jnp
from jax import lax
from jax.experimental import pallas as pl
from jax.experimental.pallas import tpu as pltpu
from jax.sharding import PartitionSpec as P

PLANE = 4
NONE = -512.0
BF = jnp.bfloat16
F32 = jnp.float32
MESH = pl.DeviceIdType.MESH


def up16(count):
    return -(-count // 16) * 16


def dot(a, b):
    return jnp.dot(a, b, preferred_element_type=F32)


def dot_t(a, b):
    return lax.dot_general(a, b, (((1,), (1,)), ((), ())), preferred_element_type=F32)


def t_dot(a, b):
    return lax.dot_general(a, b, (((0,), (0,)), ((), ())), preferred_element_type=F32)


def iota(shape, dim):
    return lax.broadcasted_iota(jnp.int32, shape, dim)


def kernel(
    depth, experts, cap_f, cap_b,
    routes_f, gates_f, routes_b, gates_b, tok_f, tok_b, grad_b, w_in, w_down,
    out_f, out_b,
    blocks, send_d, recv_d, send_t, recv_t, send_r, recv_r, send_p, recv_p,
    mine, acc, own_f, own_b, wi, wd, order, packing,
    sem_load, sem_ws, sem_wr, sem_gs, sem_gr, sem_ds, sem_dr, sem_ts, sem_tr, sem_rs, sem_rr, sem_ps, sem_pr,
):
    nf, width = tok_f.shape
    nb = tok_b.shape[0]
    half = w_down.shape[0]
    whole = (cap_f + 2 * cap_b) // 16 * 16
    rest = cap_f + 2 * cap_b - whole
    folds = width // 128
    rt = folds * rest
    mf, mb = up16(PLANE * cap_f), up16(PLANE * cap_b)
    rr = up16(cap_f + cap_b)
    sec = lax.axis_index("section")
    me = lax.axis_index("expert")
    c = me % 2
    p = (me // 2) % PLANE
    z = me // (2 * PLANE)

    def dev(zz, pp, cc):
        return (sec, (zz * PLANE + pp) * 2 + cc)

    row_b, row_g, row_f = experts, experts + nb, experts + 2 * nb
    loads = [
        pltpu.make_async_copy(tok_b, blocks.at[z, pl.ds(row_b, nb)], sem_load.at[0]),
        pltpu.make_async_copy(grad_b, blocks.at[z, pl.ds(row_g, nb)], sem_load.at[1]),
        pltpu.make_async_copy(tok_f, blocks.at[z, pl.ds(row_f, nf)], sem_load.at[2]),
        pltpu.make_async_copy(w_in, wi.at[c], sem_load.at[3]),
        pltpu.make_async_copy(w_down, wd.at[c], sem_load.at[4]),
    ]
    for load in loads:
        load.start()

    barrier = pltpu.get_barrier_semaphore()
    pl.semaphore_signal(barrier, inc=1, device_id=dev(z, p, 1 - c), device_id_type=MESH)
    for q in range(1, PLANE):
        pl.semaphore_signal(
            barrier, inc=1, device_id=dev(z, (p + q) % PLANE, c), device_id_type=MESH
        )
    for q in range(1, depth):
        pl.semaphore_signal(
            barrier, inc=1, device_id=dev((z + q) % depth, p, c), device_id_type=MESH
        )

    for load in loads[:3]:
        load.wait()
    lanes = 256
    blocks[z, 0:experts, :] = jnp.zeros((experts, width), BF)
    for routes, gates, lane in ((routes_f, gates_f, 0), (routes_b, gates_b, 128)):
        count = routes.shape[2]
        e_ids = iota((experts, count), 0)
        named = jnp.zeros((experts, count), F32)
        weight = jnp.zeros((experts, count), F32)
        for k in range(routes.shape[0]):
            hit = routes[k] == e_ids
            named = named + jnp.where(hit, 1.0, 0.0)
            weight = weight + jnp.where(hit, gates[k], 0.0)
        earlier = jnp.where(iota((count, count), 0) < iota((count, count), 1), 1.0, 0.0)
        rank = dot(named.astype(BF), earlier.astype(BF))
        high = weight.astype(BF)
        low = (weight - high.astype(F32)).astype(BF)
        code = jnp.where(named > 0.0, rank, NONE).astype(BF)
        for part, values in enumerate((code, high, low)):
            start = part * lanes + lane
            blocks[z, 0:experts, start : start + count] = values

    weight_copies = [
        pltpu.make_async_remote_copy(
            wi.at[c], wi.at[c], sem_ws.at[0], sem_wr.at[0], device_id=dev(z, p, 1 - c), device_id_type=MESH
        ),
        pltpu.make_async_remote_copy(
            wd.at[c], wd.at[c], sem_ws.at[1], sem_wr.at[1], device_id=dev(z, p, 1 - c), device_id_type=MESH
        ),
    ]
    def source(k):
        near = jnp.minimum(z, depth - 1 - z)
        side = jnp.where(k % 2 == 1, z - (k + 1) // 2, z + k // 2)
        far = jnp.where(2 * z < depth, k, depth - 1 - k)
        return jnp.where(k <= 2 * near, side, far)

    def relay(zs, way):
        return pltpu.make_async_remote_copy(
            blocks.at[zs], blocks.at[zs], sem_gs.at[zs, way], sem_gr.at[zs],
            device_id=dev((z + 1 if way else z + depth - 1) % depth, p, c), device_id_type=MESH,
        )

    def goes_right(zs):
        return (zs <= z) & (z < depth - 1)

    def goes_left(zs):
        return (zs >= z) & (z > 0)

    def passes_through(zs):
        return (zs != z) & (goes_right(zs) | goes_left(zs))

    def send_on(zs):
        @pl.when(goes_right(zs))
        def _():
            relay(zs, 1).start()

        @pl.when(goes_left(zs))
        def _():
            relay(zs, 0).start()

    def dispatch_copy(zs, q):
        tgt = (p + q) % PLANE
        return pltpu.make_async_remote_copy(
            send_d.at[zs, tgt], recv_d.at[zs, p], sem_ds.at[zs, q], sem_dr.at[zs, p],
            device_id=dev(z, tgt, c), device_id_type=MESH,
        )

    def dispatch_arrival(zs, q):
        other = (p + q) % PLANE
        return pltpu.make_async_remote_copy(
            send_d.at[zs, other], recv_d.at[zs, other], sem_ds.at[zs, q], sem_dr.at[zs, other],
            device_id=dev(z, other, c), device_id_type=MESH,
        )

    def return_copy(zs, q):
        tgt = (p + q) % PLANE
        return pltpu.make_async_remote_copy(
            send_r.at[zs, tgt], recv_r.at[zs, p], sem_rs.at[zs, q], sem_rr.at[zs, p],
            device_id=dev(z, tgt, c), device_id_type=MESH,
        )

    def return_arrival(zs, q):
        other = (p + q) % PLANE
        return pltpu.make_async_remote_copy(
            send_r.at[zs, other], recv_r.at[zs, other], sem_rs.at[zs, q], sem_rr.at[zs, other],
            device_id=dev(z, other, c), device_id_type=MESH,
        )

    def part_copy(zs):
        return pltpu.make_async_remote_copy(
            send_p.at[zs], recv_p.at[z], sem_ps.at[zs], sem_pr.at[z],
            device_id=dev(zs, p, c), device_id_type=MESH,
        )

    def part_arrival(zs):
        return pltpu.make_async_remote_copy(
            send_p.at[zs], recv_p.at[zs], sem_ps.at[zs], sem_pr.at[zs],
            device_id=dev(zs, p, c), device_id_type=MESH,
        )

    def spread(zs, rows):
        total = PLANE * rows
        pick = jnp.where(
            iota((total, experts), 1) == z * PLANE + iota((total, experts), 0) // rows, 1.0, 0.0
        ).astype(BF)
        return dot(pick, blocks[zs, 0:experts, 0 : 3 * lanes])

    def slot(total, rows, count):
        return (iota((total, count), 0) % rows).astype(F32)

    def tail_copy(zs, q):
        tgt = (p + q) % PLANE
        return pltpu.make_async_remote_copy(
            send_t.at[zs, tgt], recv_t.at[zs, p], sem_ts.at[zs, q], sem_tr.at[zs, p],
            device_id=dev(z, tgt, c), device_id_type=MESH,
        )

    def tail_arrival(zs, q):
        other = (p + q) % PLANE
        return pltpu.make_async_remote_copy(
            send_t.at[zs, other], recv_t.at[zs, other], sem_ts.at[zs, q], sem_tr.at[zs, other],
            device_id=dev(z, other, c), device_id_type=MESH,
        )

    def one_hot(hit):
        return jnp.where(hit, 1.0, 0.0).astype(BF)

    def select(zs):
        table = spread(zs, whole)
        table_f, table_b = table[:, 0:nf], table[:, 128 : 128 + nb]
        place_f, place_b = slot(PLANE * whole, whole, nf), slot(PLANE * whole, whole, nb)
        x = blocks[zs, row_b : row_b + nb, :]
        g = blocks[zs, row_g : row_g + nb, :]
        rows = (
            dot(one_hot(table_f == place_f), blocks[zs, row_f : row_f + nf, :])
            + dot(one_hot(table_b + cap_f == place_b), x)
            + dot(one_hot(table_b + (cap_f + cap_b) == place_b), g)
        ).astype(BF)
        table_t = spread(zs, rt)[:, 128 : 128 + nb]
        place_t = (iota((PLANE * rt, nb), 0) % rest + whole).astype(F32)
        wide = dot(one_hot(table_t + (cap_f + cap_b) == place_t), g)
        fold = iota((PLANE * rt, 128), 0) % rt // rest
        tail = jnp.zeros((PLANE * rt, 128), F32)
        for q in range(folds):
            tail = tail + jnp.where(fold == q, wide[:, q * 128 : (q + 1) * 128], 0.0)
        tail = tail.astype(BF)
        for q in range(PLANE):
            send_d[zs, q] = rows[q * whole : (q + 1) * whole]
            send_t[zs, q] = tail[q * rt : (q + 1) * rt]

    def dispatch(zs):
        for q in range(1, PLANE):
            dispatch_copy(zs, q).start()
            tail_copy(zs, q).start()
        recv_d[zs, p] = send_d[zs, p]
        recv_t[zs, p] = send_t[zs, p]

    def arrange():
        for start, size, count, first in (
            (0, mf, cap_f, 0), (mf, mb, cap_b, cap_f), (mf + mb, mb, cap_b, cap_f + cap_b)
        ):
            row, col = iota((size, PLANE * whole), 0), iota((size, PLANE * whole), 1)
            hit = (row // count == col // whole) & (row % count + first == col % whole)
            order[start : start + size] = one_hot(hit)
        for start, size, count, first in ((0, mf, cap_f, 0), (mf, mb, cap_b, cap_f)):
            shape = (PLANE * rr, size)
            row, col = iota(shape, 0), iota(shape, 1)
            hit = (row // rr == col // count) & (row % rr == col % count + first)
            packing[:, start : start + size] = one_hot(hit)

    def expert(zs, is_first):
        for q in range(1, PLANE):
            dispatch_arrival(zs, q).wait_recv()
            tail_arrival(zs, q).wait_recv()
        rows = dot(order[...], recv_d[zs].reshape(PLANE * whole, width))
        tail = recv_t[zs].reshape(PLANE * rt, 128)
        fold = iota((PLANE * rt, 128), 0) % rt // rest
        wide = jnp.concatenate(
            [jnp.where(fold == q, tail, jnp.zeros_like(tail)) for q in range(folds)], axis=1
        )
        row, col = iota((mb, PLANE * rt), 0), iota((mb, PLANE * rt), 1)
        hit = (row // cap_b == col // rt) & (
            row % cap_b + (cap_f + cap_b) == col % rest + whole
        )
        mine[0 : mf + mb] = rows[0 : mf + mb].astype(BF)
        mine[mf + mb :] = (rows[mf + mb :] + dot(one_hot(hit), wide)).astype(BF)

        def one_half(i, carry):
            h = (c + i) % 2

            @pl.when(is_first & (i == 1))
            def _():
                for copy in weight_copies:
                    copy.wait_recv()

            hidden = dot(mine[0 : mf + mb], wi[h])
            a, b = hidden[:, :half], hidden[:, half:]
            q = jax.nn.sigmoid(a)
            active = (a[:mf] * q[:mf] * b[:mf]).astype(BF)
            part_f = dot(active, wd[h])
            u = dot_t(mine[mf + mb : mf + 2 * mb], wd[h])
            a, b, q = a[mf:], b[mf:], q[mf:]
            grad = jnp.concatenate([u * b * q * (1.0 + a * (1.0 - q)), u * a * q], axis=1)
            part_b = dot_t(grad.astype(BF), wi[h])

            @pl.when(i == 0)
            def _():
                acc[0:mf] = part_f
                acc[mf : mf + mb] = part_b

            @pl.when(i == 1)
            def _():
                acc[0:mf] = acc[0:mf] + part_f
                acc[mf : mf + mb] = acc[mf : mf + mb] + part_b

            return carry

        lax.fori_loop(0, 2, one_half, 0)
        packed = dot(packing[...], acc[...].astype(BF)).astype(BF)
        for j in range(PLANE):
            send_r[zs, j] = packed[j * rr : (j + 1) * rr]
        for q in range(1, PLANE):
            return_copy(zs, q).start()
        recv_r[zs, p] = send_r[zs, p]

    def weigh(table, place, rows, count, lane):
        hit = table[:, lane : lane + count] == place
        high_part = jnp.where(hit, table[:, lanes + lane : lanes + lane + count], 0.0)
        low_part = jnp.where(hit, table[:, 2 * lanes + lane : 2 * lanes + lane + count], 0.0)
        return t_dot(high_part.astype(BF), rows) + t_dot(low_part.astype(BF), rows)

    def combine(zs):
        for q in range(1, PLANE):
            return_arrival(zs, q).wait_recv()
        rows = recv_r[zs].reshape(PLANE * rr, width)
        table = spread(zs, rr)
        part_f = weigh(table, slot(PLANE * rr, rr, nf), rows, nf, 0)
        part_b = weigh(table, slot(PLANE * rr, rr, nb) - cap_f, rows, nb, 128)

        @pl.when(zs == z)
        def _():
            own_f[...] = part_f
            own_b[...] = part_b

        @pl.when(zs != z)
        def _():
            send_p[zs, 0:nf, :] = part_f.astype(BF)
            send_p[zs, nf : nf + nb, :] = part_b.astype(BF)
            part_copy(zs).start()

    def pass_on(zs):
        @pl.when(passes_through(zs))
        def _():
            relay(zs, 0).wait_recv()
            send_on(zs)

    def step(k, carry):
        @pl.when(k < depth)
        def _():
            zs = source(k)

            @pl.when(jnp.logical_not(passes_through(zs)))
            def _():
                relay(zs, 0).wait_recv()

            select(zs)
            dispatch(zs)

        @pl.when(k < depth - 1)
        def _():
            pass_on(source(k + 1))

        @pl.when((k >= 2) & (k <= depth + 1))
        def _():
            expert(source((k - 1) % depth), k == 2)

        @pl.when(k >= 3)
        def _():
            combine(source((k - 2) % depth))

        return carry

    select(z)
    pl.semaphore_wait(barrier, 1 + (PLANE - 1) + (depth - 1))
    send_on(z)
    dispatch(z)
    for load, copy in zip(loads[3:], weight_copies):
        load.wait()
        copy.start()
    arrange()
    pass_on(source(1))
    lax.fori_loop(1, depth + 3, step, 0)

    total_f = blocks[z, row_f : row_f + nf, :].astype(F32)
    total_b = blocks[z, row_g : row_g + nb, :].astype(F32)
    for q in range(1, depth):
        zs = (z + q) % depth
        part_arrival(zs).wait_recv()
        total_f = total_f + recv_p[zs, 0:nf, :].astype(F32)
        total_b = total_b + recv_p[zs, nf : nf + nb, :].astype(F32)
    out_f[...] = (total_f + own_f[...]).astype(BF)
    out_b[...] = (total_b + own_b[...]).astype(BF)

    for copy in weight_copies:
        copy.wait_send()

    def drain(zs, carry):
        @pl.when(goes_right(zs))
        def _():
            relay(zs, 1).wait_send()

        @pl.when(goes_left(zs))
        def _():
            relay(zs, 0).wait_send()

        for q in range(1, PLANE):
            dispatch_copy(zs, q).wait_send()
            tail_copy(zs, q).wait_send()
            return_copy(zs, q).wait_send()

        @pl.when(zs != z)
        def _():
            part_copy(zs).wait_send()

        return carry

    lax.fori_loop(0, depth, drain, 0)


def passed_along(block, axis, distance):
    count = lax.axis_size(axis)
    if count == 1:
        return block
    route = [((i - distance) % count, i) for i in range(count)]
    return lax.ppermute(block, axis, route)


def on_device(
    forward_input, forward_routes, forward_gates,
    backward_input, backward_routes, backward_gates,
    output_grad, weight_in, weight_down,
):
    devices = lax.axis_size("expert")
    experts = devices // 2
    depth = experts // PLANE
    nf, width = forward_input.shape[1:]
    nb = backward_input.shape[1]
    half = weight_down.shape[2]
    cap_f = 2 * (7 * nf // (2 * experts))
    cap_b = 2 * (7 * nb // (2 * experts))
    whole = (cap_f + 2 * cap_b) // 16 * 16
    rt = (cap_f + 2 * cap_b - whole) * (width // 128)
    mf, mb = up16(PLANE * cap_f), up16(PLANE * cap_b)
    rr = up16(cap_f + cap_b)
    tables = [
        jnp.transpose(array, (2, 0, 1))
        for array in (forward_routes, forward_gates, backward_routes, backward_gates)
    ]
    vmem = pl.BlockSpec(memory_space=pltpu.VMEM)
    anywhere = pl.BlockSpec(memory_space=pl.ANY)
    dma = pltpu.SemaphoreType.DMA
    ahead, back = pl.pallas_call(
        functools.partial(kernel, depth, experts, cap_f, cap_b),
        out_shape=(
            jax.ShapeDtypeStruct((nf, width), BF),
            jax.ShapeDtypeStruct((nb, width), BF),
        ),
        in_specs=[vmem] * 4 + [anywhere] * 5,
        out_specs=(vmem, vmem),
        scratch_shapes=[
            pltpu.VMEM((depth, experts + 2 * nb + nf, width), BF),
            pltpu.VMEM((depth, PLANE, whole, width), BF),
            pltpu.VMEM((depth, PLANE, whole, width), BF),
            pltpu.VMEM((depth, PLANE, rt, 128), BF),
            pltpu.VMEM((depth, PLANE, rt, 128), BF),
            pltpu.VMEM((depth, PLANE, rr, width), BF),
            pltpu.VMEM((depth, PLANE, rr, width), BF),
            pltpu.VMEM((depth, nf + nb, width), BF),
            pltpu.VMEM((depth, nf + nb, width), BF),
            pltpu.VMEM((mf + 2 * mb, width), BF),
            pltpu.VMEM((mf + mb, width), F32),
            pltpu.VMEM((nf, width), F32),
            pltpu.VMEM((nb, width), F32),
            pltpu.VMEM((2, width, 2 * half), BF),
            pltpu.VMEM((2, half, width), BF),
            pltpu.VMEM((mf + 2 * mb, PLANE * whole), BF),
            pltpu.VMEM((PLANE * rr, mf + mb), BF),
            dma((5,)),
            dma((2,)),
            dma((2,)),
            dma((depth, 2)),
            dma((depth,)),
            dma((depth, PLANE)),
            dma((depth, PLANE)),
            dma((depth, PLANE)),
            dma((depth, PLANE)),
            dma((depth, PLANE)),
            dma((depth, PLANE)),
            dma((depth,)),
            dma((depth,)),
        ],
        compiler_params=pltpu.CompilerParams(
            collective_id=0, has_side_effects=True, vmem_limit_bytes=56 * 1024 * 1024
        ),
    )(
        *tables, forward_input[0], backward_input[0], output_grad[0],
        weight_in[0, 0], weight_down[0, 0],
    )
    forward_sent = passed_along(ahead[None], "section", 1)
    backward_sent = passed_along(back[None], "section", -1)
    return (forward_sent, backward_sent)


def solution(mesh):
    rows = P("section", "expert", None)
    weights = P("section", "expert", None, None)
    return jax.shard_map(
        on_device,
        mesh=mesh,
        in_specs=(rows,) * 7 + (weights,) * 2,
        out_specs=(rows, rows),
        check_vma=False,
    )
```

```python
import functools
import jax
import jax.numpy as jnp
from jax import lax
from jax.experimental import pallas as pl
from jax.experimental.pallas import tpu as pltpu
from jax.sharding import PartitionSpec as P

PLANE = 4
NONE = -512.0
BF = jnp.bfloat16
F32 = jnp.float32
MESH = pl.DeviceIdType.MESH


def up16(count):
    return -(-count // 16) * 16


def dot(a, b):
    return jnp.dot(a, b, preferred_element_type=F32)


def dot_t(a, b):
    return lax.dot_general(a, b, (((1,), (1,)), ((), ())), preferred_element_type=F32)


def t_dot(a, b):
    return lax.dot_general(a, b, (((0,), (0,)), ((), ())), preferred_element_type=F32)


def iota(shape, dim):
    return lax.broadcasted_iota(jnp.int32, shape, dim)


def kernel(
    depth, experts, cap_f, cap_b,
    routes_f, gates_f, routes_b, gates_b, tok_f, tok_b, grad_b, w_in, w_down,
    out_f, out_b,
    blocks, send_d, recv_d, send_t, recv_t, send_r, recv_r, send_p, recv_p,
    mine, acc, own_f, own_b, wi, wd, order, packing,
    sem_load, sem_ws, sem_wr, sem_gs, sem_gr, sem_ds, sem_dr, sem_ts, sem_tr, sem_rs, sem_rr, sem_ps, sem_pr,
):
    nf, width = tok_f.shape
    nb = tok_b.shape[0]
    half = w_down.shape[0]
    whole = (cap_f + 2 * cap_b) // 16 * 16
    rest = cap_f + 2 * cap_b - whole
    folds = width // 128
    rt = folds * rest
    mf, mb = up16(PLANE * cap_f), up16(PLANE * cap_b)
    rr = up16(cap_f + cap_b)
    sec = lax.axis_index("section")
    me = lax.axis_index("expert")
    c = me % 2
    p = (me // 2) % PLANE
    z = me // (2 * PLANE)

    def dev(zz, pp, cc):
        return (sec, (zz * PLANE + pp) * 2 + cc)

    row_b, row_g, row_f = experts, experts + nb, experts + 2 * nb
    loads = [
        pltpu.make_async_copy(tok_b, blocks.at[z, pl.ds(row_b, nb)], sem_load.at[0]),
        pltpu.make_async_copy(grad_b, blocks.at[z, pl.ds(row_g, nb)], sem_load.at[1]),
        pltpu.make_async_copy(tok_f, blocks.at[z, pl.ds(row_f, nf)], sem_load.at[2]),
        pltpu.make_async_copy(w_in, wi.at[c], sem_load.at[3]),
        pltpu.make_async_copy(w_down, wd.at[c], sem_load.at[4]),
    ]
    for load in loads:
        load.start()

    barrier = pltpu.get_barrier_semaphore()
    pl.semaphore_signal(barrier, inc=1, device_id=dev(z, p, 1 - c), device_id_type=MESH)
    for q in range(1, PLANE):
        pl.semaphore_signal(
            barrier, inc=1, device_id=dev(z, (p + q) % PLANE, c), device_id_type=MESH
        )
    for q in range(1, depth):
        pl.semaphore_signal(
            barrier, inc=1, device_id=dev((z + q) % depth, p, c), device_id_type=MESH
        )

    for load in loads[:3]:
        load.wait()
    lanes = 256
    blocks[z, 0:experts, :] = jnp.zeros((experts, width), BF)
    for routes, gates, lane in ((routes_f, gates_f, 0), (routes_b, gates_b, 128)):
        count = routes.shape[2]
        e_ids = iota((experts, count), 0)
        named = jnp.zeros((experts, count), F32)
        weight = jnp.zeros((experts, count), F32)
        for k in range(routes.shape[0]):
            hit = routes[k] == e_ids
            named = named + jnp.where(hit, 1.0, 0.0)
            weight = weight + jnp.where(hit, gates[k], 0.0)
        earlier = jnp.where(iota((count, count), 0) < iota((count, count), 1), 1.0, 0.0)
        rank = dot(named.astype(BF), earlier.astype(BF))
        high = weight.astype(BF)
        low = (weight - high.astype(F32)).astype(BF)
        code = jnp.where(named > 0.0, rank, NONE).astype(BF)
        for part, values in enumerate((code, high, low)):
            start = part * lanes + lane
            blocks[z, 0:experts, start : start + count] = values

    weight_copies = [
        pltpu.make_async_remote_copy(
            wi.at[c], wi.at[c], sem_ws.at[0], sem_wr.at[0], device_id=dev(z, p, 1 - c), device_id_type=MESH
        ),
        pltpu.make_async_remote_copy(
            wd.at[c], wd.at[c], sem_ws.at[1], sem_wr.at[1], device_id=dev(z, p, 1 - c), device_id_type=MESH
        ),
    ]
    def source(k):
        near = jnp.minimum(z, depth - 1 - z)
        side = jnp.where(k % 2 == 1, z - (k + 1) // 2, z + k // 2)
        far = jnp.where(2 * z < depth, k, depth - 1 - k)
        return jnp.where(k <= 2 * near, side, far)

    def relay(zs, way):
        return pltpu.make_async_remote_copy(
            blocks.at[zs], blocks.at[zs], sem_gs.at[zs, way], sem_gr.at[zs],
            device_id=dev((z + 1 if way else z + depth - 1) % depth, p, c), device_id_type=MESH,
        )

    def goes_right(zs):
        return (zs <= z) & (z < depth - 1)

    def goes_left(zs):
        return (zs >= z) & (z > 0)

    def passes_through(zs):
        return (zs != z) & (goes_right(zs) | goes_left(zs))

    def send_on(zs):
        @pl.when(goes_right(zs))
        def _():
            relay(zs, 1).start()

        @pl.when(goes_left(zs))
        def _():
            relay(zs, 0).start()

    def dispatch_copy(zs, q):
        tgt = (p + q) % PLANE
        return pltpu.make_async_remote_copy(
            send_d.at[zs, tgt], recv_d.at[zs, p], sem_ds.at[zs, q], sem_dr.at[zs, p],
            device_id=dev(z, tgt, c), device_id_type=MESH,
        )

    def dispatch_arrival(zs, q):
        other = (p + q) % PLANE
        return pltpu.make_async_remote_copy(
            send_d.at[zs, other], recv_d.at[zs, other], sem_ds.at[zs, q], sem_dr.at[zs, other],
            device_id=dev(z, other, c), device_id_type=MESH,
        )

    def return_copy(zs, q):
        tgt = (p + q) % PLANE
        return pltpu.make_async_remote_copy(
            send_r.at[zs, tgt], recv_r.at[zs, p], sem_rs.at[zs, q], sem_rr.at[zs, p],
            device_id=dev(z, tgt, c), device_id_type=MESH,
        )

    def return_arrival(zs, q):
        other = (p + q) % PLANE
        return pltpu.make_async_remote_copy(
            send_r.at[zs, other], recv_r.at[zs, other], sem_rs.at[zs, q], sem_rr.at[zs, other],
            device_id=dev(z, other, c), device_id_type=MESH,
        )

    def part_copy(zs):
        return pltpu.make_async_remote_copy(
            send_p.at[zs], recv_p.at[z], sem_ps.at[zs], sem_pr.at[z],
            device_id=dev(zs, p, c), device_id_type=MESH,
        )

    def part_arrival(zs):
        return pltpu.make_async_remote_copy(
            send_p.at[zs], recv_p.at[zs], sem_ps.at[zs], sem_pr.at[zs],
            device_id=dev(zs, p, c), device_id_type=MESH,
        )

    def spread(zs, rows):
        total = PLANE * rows
        pick = jnp.where(
            iota((total, experts), 1) == z * PLANE + iota((total, experts), 0) // rows, 1.0, 0.0
        ).astype(BF)
        return dot(pick, blocks[zs, 0:experts, 0 : 3 * lanes])

    def slot(total, rows, count):
        return (iota((total, count), 0) % rows).astype(F32)

    def tail_copy(zs, q):
        tgt = (p + q) % PLANE
        return pltpu.make_async_remote_copy(
            send_t.at[zs, tgt], recv_t.at[zs, p], sem_ts.at[zs, q], sem_tr.at[zs, p],
            device_id=dev(z, tgt, c), device_id_type=MESH,
        )

    def tail_arrival(zs, q):
        other = (p + q) % PLANE
        return pltpu.make_async_remote_copy(
            send_t.at[zs, other], recv_t.at[zs, other], sem_ts.at[zs, q], sem_tr.at[zs, other],
            device_id=dev(z, other, c), device_id_type=MESH,
        )

    def one_hot(hit):
        return jnp.where(hit, 1.0, 0.0).astype(BF)

    def select(zs):
        table = spread(zs, whole)
        table_f, table_b = table[:, 0:nf], table[:, 128 : 128 + nb]
        place_f, place_b = slot(PLANE * whole, whole, nf), slot(PLANE * whole, whole, nb)
        x = blocks[zs, row_b : row_b + nb, :]
        g = blocks[zs, row_g : row_g + nb, :]
        rows = (
            dot(one_hot(table_f == place_f), blocks[zs, row_f : row_f + nf, :])
            + dot(one_hot(table_b + cap_f == place_b), x)
            + dot(one_hot(table_b + (cap_f + cap_b) == place_b), g)
        ).astype(BF)
        table_t = spread(zs, rt)[:, 128 : 128 + nb]
        place_t = (iota((PLANE * rt, nb), 0) % rest + whole).astype(F32)
        wide = dot(one_hot(table_t + (cap_f + cap_b) == place_t), g)
        fold = iota((PLANE * rt, 128), 0) % rt // rest
        tail = jnp.zeros((PLANE * rt, 128), F32)
        for q in range(folds):
            tail = tail + jnp.where(fold == q, wide[:, q * 128 : (q + 1) * 128], 0.0)
        tail = tail.astype(BF)
        for q in range(PLANE):
            send_d[zs, q] = rows[q * whole : (q + 1) * whole]
            send_t[zs, q] = tail[q * rt : (q + 1) * rt]

    def dispatch(zs):
        for q in range(1, PLANE):
            dispatch_copy(zs, q).start()
            tail_copy(zs, q).start()
        recv_d[zs, p] = send_d[zs, p]
        recv_t[zs, p] = send_t[zs, p]

    def arrange():
        for start, size, count, first in (
            (0, mf, cap_f, 0), (mf, mb, cap_b, cap_f), (mf + mb, mb, cap_b, cap_f + cap_b)
        ):
            row, col = iota((size, PLANE * whole), 0), iota((size, PLANE * whole), 1)
            hit = (row // count == col // whole) & (row % count + first == col % whole)
            order[start : start + size] = one_hot(hit)
        for start, size, count, first in ((0, mf, cap_f, 0), (mf, mb, cap_b, cap_f)):
            shape = (PLANE * rr, size)
            row, col = iota(shape, 0), iota(shape, 1)
            hit = (row // rr == col // count) & (row % rr == col % count + first)
            packing[:, start : start + size] = one_hot(hit)

    def gather_rows(zs):
        for q in range(1, PLANE):
            dispatch_arrival(zs, q).wait_recv()
            tail_arrival(zs, q).wait_recv()
        rows = dot(order[...], recv_d[zs].reshape(PLANE * whole, width))
        tail = recv_t[zs].reshape(PLANE * rt, 128)
        fold = iota((PLANE * rt, 128), 0) % rt // rest
        wide = jnp.concatenate(
            [jnp.where(fold == q, tail, jnp.zeros_like(tail)) for q in range(folds)], axis=1
        )
        row, col = iota((mb, PLANE * rt), 0), iota((mb, PLANE * rt), 1)
        hit = (row // cap_b == col // rt) & (
            row % cap_b + (cap_f + cap_b) == col % rest + whole
        )
        mine[zs, 0 : mf + mb] = rows[0 : mf + mb].astype(BF)
        mine[zs, mf + mb :] = (rows[mf + mb :] + dot(one_hot(hit), wide)).astype(BF)

    def work(zs, h):
        hidden = dot(mine[zs, 0 : mf + mb], wi[h])
        a, b = hidden[:, :half], hidden[:, half:]
        q = jax.nn.sigmoid(a)
        active = (a[:mf] * q[:mf] * b[:mf]).astype(BF)
        part_f = dot(active, wd[h])
        u = dot_t(mine[zs, mf + mb : mf + 2 * mb], wd[h])
        a, b, q = a[mf:], b[mf:], q[mf:]
        grad = jnp.concatenate([u * b * q * (1.0 + a * (1.0 - q)), u * a * q], axis=1)
        part_b = dot_t(grad.astype(BF), wi[h])
        return part_f, part_b

    def own_half(zs):
        gather_rows(zs)
        part_f, part_b = work(zs, c)
        acc[zs, 0:mf] = part_f
        acc[zs, mf : mf + mb] = part_b

    def other_half(zs):
        part_f, part_b = work(zs, 1 - c)
        acc[zs, 0:mf] = acc[zs, 0:mf] + part_f
        acc[zs, mf : mf + mb] = acc[zs, mf : mf + mb] + part_b
        packed = dot(packing[...], acc[zs].astype(BF)).astype(BF)
        for j in range(PLANE):
            send_r[zs, j] = packed[j * rr : (j + 1) * rr]
        for q in range(1, PLANE):
            return_copy(zs, q).start()
        recv_r[zs, p] = send_r[zs, p]

    def weigh(table, place, rows, count, lane):
        hit = table[:, lane : lane + count] == place
        high_part = jnp.where(hit, table[:, lanes + lane : lanes + lane + count], 0.0)
        low_part = jnp.where(hit, table[:, 2 * lanes + lane : 2 * lanes + lane + count], 0.0)
        return t_dot(high_part.astype(BF), rows) + t_dot(low_part.astype(BF), rows)

    def combine(zs):
        for q in range(1, PLANE):
            return_arrival(zs, q).wait_recv()
        rows = recv_r[zs].reshape(PLANE * rr, width)
        table = spread(zs, rr)
        part_f = weigh(table, slot(PLANE * rr, rr, nf), rows, nf, 0)
        part_b = weigh(table, slot(PLANE * rr, rr, nb) - cap_f, rows, nb, 128)

        @pl.when(zs == z)
        def _():
            own_f[...] = part_f
            own_b[...] = part_b

        @pl.when(zs != z)
        def _():
            send_p[zs, 0:nf, :] = part_f.astype(BF)
            send_p[zs, nf : nf + nb, :] = part_b.astype(BF)
            part_copy(zs).start()

    def pass_on(zs):
        @pl.when(passes_through(zs))
        def _():
            relay(zs, 0).wait_recv()
            send_on(zs)

    def step(k, carry):
        @pl.when(k < depth)
        def _():
            zs = source(k)

            @pl.when(jnp.logical_not(passes_through(zs)))
            def _():
                relay(zs, 0).wait_recv()

            select(zs)
            dispatch(zs)

        @pl.when(k < depth - 1)
        def _():
            pass_on(source(k + 1))

        @pl.when(k == 3)
        def _():
            for copy in weight_copies:
                copy.wait_recv()

        @pl.when((k >= 3) & (k <= depth + 2))
        def _():
            other_half(source((k - 2) % depth))

        @pl.when(k >= 4)
        def _():
            combine(source((k - 3) % depth))

        @pl.when(k <= depth)
        def _():
            own_half(source(k - 1))

        return carry

    select(z)
    pl.semaphore_wait(barrier, 1 + (PLANE - 1) + (depth - 1))
    send_on(z)
    dispatch(z)
    for load, copy in zip(loads[3:], weight_copies):
        load.wait()
        copy.start()
    arrange()
    pass_on(source(1))
    lax.fori_loop(1, depth + 4, step, 0)

    total_f = blocks[z, row_f : row_f + nf, :].astype(F32)
    total_b = blocks[z, row_g : row_g + nb, :].astype(F32)
    for q in range(1, depth):
        zs = (z + q) % depth
        part_arrival(zs).wait_recv()
        total_f = total_f + recv_p[zs, 0:nf, :].astype(F32)
        total_b = total_b + recv_p[zs, nf : nf + nb, :].astype(F32)
    out_f[...] = (total_f + own_f[...]).astype(BF)
    out_b[...] = (total_b + own_b[...]).astype(BF)

    for copy in weight_copies:
        copy.wait_send()

    def drain(zs, carry):
        @pl.when(goes_right(zs))
        def _():
            relay(zs, 1).wait_send()

        @pl.when(goes_left(zs))
        def _():
            relay(zs, 0).wait_send()

        for q in range(1, PLANE):
            dispatch_copy(zs, q).wait_send()
            tail_copy(zs, q).wait_send()
            return_copy(zs, q).wait_send()

        @pl.when(zs != z)
        def _():
            part_copy(zs).wait_send()

        return carry

    lax.fori_loop(0, depth, drain, 0)


def passed_along(block, axis, distance):
    count = lax.axis_size(axis)
    if count == 1:
        return block
    route = [((i - distance) % count, i) for i in range(count)]
    return lax.ppermute(block, axis, route)


def on_device(
    forward_input, forward_routes, forward_gates,
    backward_input, backward_routes, backward_gates,
    output_grad, weight_in, weight_down,
):
    devices = lax.axis_size("expert")
    experts = devices // 2
    depth = experts // PLANE
    nf, width = forward_input.shape[1:]
    nb = backward_input.shape[1]
    half = weight_down.shape[2]
    cap_f = 2 * (7 * nf // (2 * experts))
    cap_b = 2 * (7 * nb // (2 * experts))
    whole = (cap_f + 2 * cap_b) // 16 * 16
    rt = (cap_f + 2 * cap_b - whole) * (width // 128)
    mf, mb = up16(PLANE * cap_f), up16(PLANE * cap_b)
    rr = up16(cap_f + cap_b)
    tables = [
        jnp.transpose(array, (2, 0, 1))
        for array in (forward_routes, forward_gates, backward_routes, backward_gates)
    ]
    vmem = pl.BlockSpec(memory_space=pltpu.VMEM)
    anywhere = pl.BlockSpec(memory_space=pl.ANY)
    dma = pltpu.SemaphoreType.DMA
    ahead, back = pl.pallas_call(
        functools.partial(kernel, depth, experts, cap_f, cap_b),
        out_shape=(
            jax.ShapeDtypeStruct((nf, width), BF),
            jax.ShapeDtypeStruct((nb, width), BF),
        ),
        in_specs=[vmem] * 4 + [anywhere] * 5,
        out_specs=(vmem, vmem),
        scratch_shapes=[
            pltpu.VMEM((depth, experts + 2 * nb + nf, width), BF),
            pltpu.VMEM((depth, PLANE, whole, width), BF),
            pltpu.VMEM((depth, PLANE, whole, width), BF),
            pltpu.VMEM((depth, PLANE, rt, 128), BF),
            pltpu.VMEM((depth, PLANE, rt, 128), BF),
            pltpu.VMEM((depth, PLANE, rr, width), BF),
            pltpu.VMEM((depth, PLANE, rr, width), BF),
            pltpu.VMEM((depth, nf + nb, width), BF),
            pltpu.VMEM((depth, nf + nb, width), BF),
            pltpu.VMEM((depth, mf + 2 * mb, width), BF),
            pltpu.VMEM((depth, mf + mb, width), F32),
            pltpu.VMEM((nf, width), F32),
            pltpu.VMEM((nb, width), F32),
            pltpu.VMEM((2, width, 2 * half), BF),
            pltpu.VMEM((2, half, width), BF),
            pltpu.VMEM((mf + 2 * mb, PLANE * whole), BF),
            pltpu.VMEM((PLANE * rr, mf + mb), BF),
            dma((5,)),
            dma((2,)),
            dma((2,)),
            dma((depth, 2)),
            dma((depth,)),
            dma((depth, PLANE)),
            dma((depth, PLANE)),
            dma((depth, PLANE)),
            dma((depth, PLANE)),
            dma((depth, PLANE)),
            dma((depth, PLANE)),
            dma((depth,)),
            dma((depth,)),
        ],
        compiler_params=pltpu.CompilerParams(
            collective_id=0, has_side_effects=True, vmem_limit_bytes=56 * 1024 * 1024
        ),
    )(
        *tables, forward_input[0], backward_input[0], output_grad[0],
        weight_in[0, 0], weight_down[0, 0],
    )
    forward_sent = passed_along(ahead[None], "section", 1)
    backward_sent = passed_along(back[None], "section", -1)
    return (forward_sent, backward_sent)


def solution(mesh):
    rows = P("section", "expert", None)
    weights = P("section", "expert", None, None)
    return jax.shard_map(
        on_device,
        mesh=mesh,
        in_specs=(rows,) * 7 + (weights,) * 2,
        out_specs=(rows, rows),
        check_vma=False,
    )
```
